512 devices in a mesh: dp: 64 (over y, z_lo, core), hd: 8 (over z_hi, x).
Axes of the slice: x: 4, y: 4, z: 16 (z_hi: 2, z_lo: 8; z = z_hi * 8 + z_lo), core: 2. Of those that a mesh axis runs over, the one named last changes fastest.
Arguments:
- query: bfloat16 [256, 2, 64, 576], P('dp', None, 'hd')
- cache: bfloat16 [256, 192, 576], P('dp')
- lengths: int32 [256], P('dp'), may hold values from 2 to 192
- counts: int32 [64], P('dp'), may hold values from 1 to 4
- value_up: bfloat16 [64, 512, 128], P('hd'), may hold values from -0.25 to 0.25
- out_proj: bfloat16 [8192, 7168], P('hd', 'dp'), may hold values from -0.25 to 0.25
- residual: bfloat16 [512, 7168], P('dp', 'hd'), may hold values from -6 to 6
- norm_gain: float32 [7168], P('hd'), may hold values from 0.25 to 1.75
- gate_weight: bfloat16 [7168, 18432], P('hd', 'dp'), may hold values from -0.0625 to 0.0625
- up_weight: bfloat16 [7168, 18432], P('hd', 'dp'), may hold values from -0.0625 to 0.0625
- down_weight: bfloat16 [18432, 7168], P('dp', 'hd'), may hold values from -0.046875 to 0.046875
Outputs:
- layer_out: bfloat16 [512, 7168], P('dp', 'hd')
The draws below stay inside these ranges and needn't reach their ends.
All inputs are finite; a program needn't handle non-finite values.
Results may differ from the reference program's by a relative error of at most 0.015.
Values may be sent and summed in bfloat16 or wider, within the bound.
A program may use at most 64 MiB of HBM per device.

```python
import jax
import jax.numpy as jnp
from jax import lax

D = 7168
FF = 18432
HEADS = 64
LAT = 512
ROPE = 64
VHEAD = 128
QTOK = 2
SLOTS = 4
CACHE = 192
REQS = 256
TOKENS = 512
N_DP = 64


def cache_values(key):
    base = jax.random.normal(key, (REQS, CACHE, LAT + ROPE), jnp.float32)
    return jnp.clip(base, -5.0, 5.0)


def draw_cache(key, part):
    values = cache_values(key)
    return values.astype(jnp.bfloat16)


def draw_query(key, part):
    key = jax.random.fold_in(key, 11)
    first = jax.random.fold_in(key, 0)
    drawn = jnp.clip(jax.random.normal(first, (REQS, QTOK, HEADS, LAT + ROPE), jnp.float32), -5.0, 5.0)
    return drawn.astype(jnp.bfloat16)


def draw_counts(key, part):
    key = jax.random.fold_in(key, 3)
    first, second = jax.random.split(key)
    values = jax.random.randint(first, (N_DP,), 1, SLOTS + 1)
    spot = jax.random.randint(second, (), 0, N_DP)
    return values.at[spot].set(SLOTS).astype(jnp.int32)


def draw_lengths(key, part):
    key = jax.random.fold_in(key, 5)
    first, second = jax.random.split(key)
    values = jax.random.randint(first, (REQS,), QTOK, CACHE + 1)
    spot = jax.random.randint(second, (), 0, REQS)
    return values.at[spot].set(CACHE).astype(jnp.int32)


def shard_levels(key, dims, cuts, least, high):
    gain = 1.0
    for axis_at, shards_of in cuts:
        heights = jax.random.uniform(jax.random.fold_in(jax.random.fold_in(key, 6), axis_at), (shards_of,), jnp.float32, least / len(cuts), high / len(cuts))
        gain = gain * jnp.repeat(jnp.exp(heights), dims[axis_at] // shards_of).reshape((-1,) + (1,) * (len(dims) - 1 - axis_at))
    return gain


def noise(stream_key, shape, width, most, cuts=(), held_as=jnp.bfloat16):
    drawn = width * jax.random.normal(stream_key, shape, jnp.float32)
    if cuts:
        drawn = drawn * shard_levels(stream_key, shape, cuts, -0.22, 0.18)
    return jnp.clip(drawn, -most, most).astype(held_as)


def setup_inputs(seed: int = 0) -> dict:
    arg_keys = jax.random.split(jax.random.key(seed), 12)
    query = draw_query(jax.random.fold_in(arg_keys[11], 71), 0)
    cache = draw_cache(jax.random.fold_in(arg_keys[11], 71), 0)
    lengths = draw_lengths(jax.random.fold_in(arg_keys[11], 71), 0)
    counts = draw_counts(jax.random.fold_in(arg_keys[11], 71), 0)
    value_up = noise(arg_keys[4], (HEADS, LAT, VHEAD), LAT ** -0.5, 0.25, ((0, 8),))
    out_proj = noise(arg_keys[5], (HEADS * VHEAD, D), (HEADS * VHEAD // 16) ** -0.5, 0.25, ((0, 8), (1, 64)))
    residual = noise(arg_keys[6], (TOKENS, D), 1.0, 6.0, ((0, 64), (1, 8)))
    norm_gain = jnp.clip(1.0 + 0.15 * jax.random.normal(arg_keys[7], (D,), jnp.float32), 0.25, 1.75)
    gate_weight = noise(arg_keys[8], (D, FF), D ** -0.5, 0.0625, ((0, 8), (1, 64)))
    up_weight = noise(arg_keys[9], (D, FF), D ** -0.5, 0.0625, ((0, 8), (1, 64)))
    down_weight = noise(arg_keys[10], (FF, D), FF ** -0.5, 0.046875, ((0, 64), (1, 8)))
    return {"query": query, "cache": cache, "lengths": lengths, "counts": counts, "value_up": value_up, "out_proj": out_proj, "residual": residual, "norm_gain": norm_gain, "gate_weight": gate_weight, "up_weight": up_weight, "down_weight": down_weight}


def attend(block):
    query, cache, lengths = block
    qf = query.astype(jnp.float32)
    cf = cache.astype(jnp.float32)
    scores = jnp.einsum('sthc,spc->sthp', qf, cf) / jnp.sqrt(jnp.float32(VHEAD + ROPE))
    limit = lengths[:, None] - QTOK + 1 + jnp.arange(QTOK, dtype=jnp.int32)[None, :]
    keep = jnp.arange(CACHE, dtype=jnp.int32)[None, None, None, :] < limit[:, :, None, None]
    scores = jnp.where(keep, scores, -1e+30)
    top = lax.optimization_barrier(jnp.max(scores, axis=-1, keepdims=True))
    expo = jnp.exp(scores - top)
    weights = (expo / lax.optimization_barrier(jnp.sum(expo, axis=-1, keepdims=True))).astype(jnp.bfloat16)
    latent = jnp.einsum('sthp,spc->sthc', weights.astype(jnp.float32), cf[:, :, :LAT])
    return latent.astype(jnp.bfloat16)

def reference(query, cache, lengths, counts, value_up, out_proj, residual, norm_gain, gate_weight, up_weight, down_weight):
    qb = query.reshape(N_DP, SLOTS, QTOK, HEADS, LAT + ROPE)
    cb = cache.reshape(N_DP, SLOTS, CACHE, LAT + ROPE)
    lb = lengths.reshape(N_DP, SLOTS)
    latent = lax.map(attend, (qb, cb, lb)).reshape(REQS, QTOK, HEADS, LAT)
    live = (jnp.arange(SLOTS, dtype=jnp.int32)[None, :] < counts[:, None]).reshape(REQS)
    livef = live.astype(jnp.float32)
    heads = jnp.einsum('rthc,hcv->rthv', latent.astype(jnp.float32), value_up.astype(jnp.float32))
    heads = (heads * livef[:, None, None, None]).astype(jnp.bfloat16)
    head_out = heads.reshape(TOKENS, HEADS * VHEAD)
    attn = jnp.dot(head_out, out_proj, preferred_element_type=jnp.float32).astype(jnp.bfloat16)
    state = (residual.astype(jnp.float32) + attn.astype(jnp.float32)).astype(jnp.bfloat16)
    statef = state.astype(jnp.float32)
    sumsq = lax.optimization_barrier(jnp.sum(statef * statef, axis=1))
    scaled = (statef * norm_gain[None, :]).astype(jnp.bfloat16)
    inverse = lax.rsqrt(sumsq / D + 1e-06)[:, None]
    gate = jnp.dot(scaled, gate_weight, preferred_element_type=jnp.float32) * inverse
    up = jnp.dot(scaled, up_weight, preferred_element_type=jnp.float32) * inverse
    hidden = (jax.nn.silu(gate) * up).astype(jnp.bfloat16)
    down = jnp.dot(hidden, down_weight, preferred_element_type=jnp.float32)
    token_live = jnp.repeat(livef, QTOK)[:, None]
    return ((statef + down) * token_live).astype(jnp.bfloat16)
```

```python
import functools

import jax
import jax.numpy as jnp
from jax import lax
from jax.experimental import pallas as pl
from jax.experimental.pallas import tpu as pltpu
from jax.sharding import PartitionSpec as P

MESH = pl.DeviceIdType.MESH
F32, BF16 = jnp.float32, jnp.bfloat16
D = 7168
SLOTS, QTOK, HEADS, LAT, QK, POS = 4, 2, 8, 512, 576, 192
NX, NY, NZ, NSEM = 4, 4, 8, 256
OUTCOL, FEAT, UNITS = 112, 896, 288


def flip(value, mask, bits=3):
    out = 0
    for i in range(bits):
        bit = lax.rem(lax.div(value, 1 << i), 2)
        out = out + (1 - bit if (mask >> i) & 1 else bit) * (1 << i)
    return out


def kernel(
    query, cache, lengths, counts, value_up, out_proj, residual, norm_gain, gate_w, up_w, down_w,
    out,
    lat, hsc, tf, g1, w1, pb, rx, sb, rz, rsp, rt, gn, st, so, g2, w2, gb, rxg, sx, rzh, hb, w3,
    dsend, drecv, eb, fr, fb, zr, osum, orx, stf, ss, rs,
):
    dp, hd = lax.axis_index("dp"), lax.axis_index("hd")
    x, zh = lax.rem(hd, NX), lax.div(hd, NX)
    c, z, y = lax.rem(dp, 2), lax.rem(lax.div(dp, 2), NZ), lax.div(dp, 2 * NZ)
    o = 1 - c

    def at(x_=x, zh_=zh, y_=y, z_=z, c_=c):
        return ((y_ * NZ + z_) * 2 + c_, zh_ * NX + x_)

    def plus(v, d, n):
        return lax.rem(v + d, n)

    used = [0]
    sent = []

    def sems(n):
        first = used[0]
        used[0] += n
        return first

    def copy(src, dst, send, recv, dev):
        return pltpu.make_async_remote_copy(
            src_ref=src, dst_ref=dst, send_sem=ss.at[send], recv_sem=rs.at[recv],
            device_id=dev, device_id_type=MESH,
        )

    def go(src, dst, sem, dev):
        cp = copy(src, dst, sem, sem, dev)
        cp.start()
        sent.append((None, cp))
        return cp

    barrier = pltpu.get_barrier_semaphore()
    partners = [at(c_=o)]
    for d in range(1, 16):
        z16 = plus(zh * NZ + z, d, 16)
        partners.append(at(zh_=lax.div(z16, NZ), z_=lax.rem(z16, NZ)))
    for d in range(1, 16):
        partners.append(at(x_=plus(x, d % 4, NX), y_=plus(y, d // 4, NY)))
    for dev in partners:
        pl.semaphore_signal(barrier, inc=1, device_id=dev, device_id_type=MESH)

    count = counts[0]
    row16 = lax.broadcasted_iota(jnp.int32, (16, POS), 0)
    pos = lax.broadcasted_iota(jnp.int32, (16, POS), 1)
    for s in range(SLOTS):
        sc = lax.dot_general(query[s], cache[s], (((1,), (1,)), ((), ())), preferred_element_type=F32)
        sc = sc * F32(192.0**-0.5)
        keep = pos < lengths[s] - 1 + jnp.where(row16 >= HEADS, 1, 0)
        sc = jnp.where(keep, sc, -1e30)
        ex = jnp.exp(sc - jnp.max(sc, axis=-1, keepdims=True))
        wt = (ex / jnp.sum(ex, axis=-1, keepdims=True)).astype(BF16)
        la = jnp.dot(wt, cache[s, :, :LAT], preferred_element_type=F32)
        la = la.astype(BF16).astype(F32)
        for k in range(4):
            lat[k, pl.ds(s * 16, 16), :] = la[:, k * 128 : (k + 1) * 128]
    row8 = lax.broadcasted_iota(jnp.int32, (8, 128), 0)
    live = jnp.where(lax.div(row8, QTOK) < count, F32(1), F32(0))
    for h in range(HEADS):
        lh = [lat[k, pl.ds(h, 8, stride=HEADS), :] for k in range(4)]
        lh = jnp.concatenate(lh, axis=1).astype(BF16)
        hv = jnp.dot(lh, value_up[h], preferred_element_type=F32) * live
        hsc[h // 4, :, (h % 4) * 128 : (h % 4 + 1) * 128] = hv.astype(BF16).astype(F32)

    res, gain = residual[...].astype(F32), norm_gain[...]
    rsp[...] = jnp.zeros_like(rsp)
    gn[...] = jnp.zeros_like(gn)
    for b in range(8):
        lo = (b // 2) * 128
        rsp[b % 2, :, lo : lo + OUTCOL] = res[:, b * OUTCOL : (b + 1) * OUTCOL]
        gn[b % 2, :, lo : lo + OUTCOL] = gain[:, b * OUTCOL : (b + 1) * OUTCOL]

    pl.semaphore_wait(barrier, len(partners))

    peer = at(c_=o)
    heads_cp = go(hsc.at[o], tf.at[c], sems(1), peer)
    res_cp = go(rsp.at[o], rt.at[c], sems(1), peer)
    tf[c] = hsc[c]
    rt[c] = rsp[c]
    heads_cp.wait_recv()
    g1[c, y, z] = tf[...].reshape(16, 512).astype(BF16)

    def gather_z(g):
        first = sems(8)
        cps = {}
        for j in (7, 6, 5, 4, 3, 2, 1):
            cps[j] = go(g.at[c, y, z], g.at[c, y, z], first + j, at(z_=flip(z, j)))
        return cps

    def gather_rest(g, cps, consume):
        ysem, csem = sems(8), sems(8)
        zg = lax.div(z, 4) * 4
        ycp, ccp = {}, {}
        for gi in range(2):
            base = zg if gi == 0 else 4 - zg
            for j in range(gi * 4 + (gi == 0), gi * 4 + 4):
                cps[j].wait_recv()
            part = g.at[c, y, pl.ds(base, 4)]
            for d in (1, 3, 2):
                ycp[d, gi] = go(part, part, ysem + gi * 4 + d, at(y_=plus(y, d, NY)))
            ccp[0, gi] = go(part, part, csem + gi * 4, peer)
        for d in (1, 3, 2):
            yd = plus(y, NY - d, NY)
            for gi in range(2):
                ycp[d, gi].wait_recv()
                part = g.at[c, yd, pl.ds(zg if gi == 0 else 4 - zg, 4)]
                ccp[d, gi] = go(part, part, csem + gi * 4 + d, peer)
        for d in (0, 1, 3, 2):
            for gi in range(2):
                ccp[d, gi].wait_recv()
            consume(plus(y, NY - d, NY), d)

    cps = gather_z(g1)

    w1[...] = jnp.zeros_like(w1)
    w1[:, :OUTCOL] = out_proj[...]
    w2[...] = jnp.zeros_like(w2)
    for b in range(8):
        lo = (b // 2) * 128
        w2[b % 2, lo : lo + OUTCOL, :UNITS] = gate_w[b * OUTCOL : (b + 1) * OUTCOL, :]
        w2[b % 2, lo : lo + OUTCOL, UNITS : 2 * UNITS] = up_w[b * OUTCOL : (b + 1) * OUTCOL, :]
    r_ = lax.broadcasted_iota(jnp.int32, (16, 128), 0)
    c_ = lax.broadcasted_iota(jnp.int32, (16, 128), 1)
    ones = jnp.where((r_ < 2) & (c_ == 64), F32(1), F32(0)).astype(BF16)
    for k in range(2):
        w2[k, OUTCOL:128, 512:640] = ones
    w3[...] = jnp.zeros_like(w3)
    w3[0, :UNITS, :] = down_w[:, :512]
    w3[1, :UNITS, :384] = down_w[:, 512:]
    hb[...] = jnp.zeros_like(hb)

    xt = lax.rem(y, 2) * 2 + lax.div(z, 4)
    here = x == xt
    slot = lax.div(y, 2) * 4 + x
    psend, precv = sems(4), sems(8)
    slot_sem = precv + slot

    def out_projection(yd, d):
        left, right = g1[0, yd].reshape(128, 512), g1[1, yd].reshape(128, 512)
        pv = jnp.dot(left, w1[:512, :], preferred_element_type=F32)
        pv = pv + jnp.dot(right, w1[512:, :], preferred_element_type=F32)
        pb[yd] = pv.astype(BF16).reshape(NZ, 16, 128)
        cp = copy(pb.at[yd], rx.at[slot], psend + d, slot_sem, at(x_=xt, y_=yd))
        if d == 0:

            @pl.when(jnp.logical_not(here))
            def _():
                cp.start()

            @pl.when(here)
            def _():
                rx[slot] = pb[yd]

            sent.append((jnp.logical_not(here), cp))
        else:
            cp.start()
            sent.append((None, cp))

    gather_rest(g1, cps, out_projection)

    holder = lax.rem(x, 2) == lax.div(z, 4)
    own = jnp.logical_and(holder, lax.rem(y, 2) == lax.div(x, 2))
    zsend, zrecv = sems(16), sems(8)
    z16 = zh * NZ + z
    myslot = zh * 4 + lax.rem(z, 4)
    to_z = []
    for d in range(1, 16):
        t = plus(z16, d, 16)
        dev = at(zh_=lax.div(t, NZ), z_=lax.rem(t, NZ))
        to_z.append(copy(sb.at[t], rz.at[myslot], zsend + d, zrecv + myslot, dev))

    @pl.when(holder)
    def _():
        for i in range(8):
            is_self = jnp.logical_and(own, slot == i)

            @pl.when(jnp.logical_not(is_self))
            def _():
                copy(rx.at[i], rx.at[i], psend, precv + i, peer).wait_recv()

        for k in range(2):
            tot = rx[4 * k].astype(F32) + rx[4 * k + 1].astype(F32)
            tot = tot + rx[4 * k + 2].astype(F32) + rx[4 * k + 3].astype(F32)
            sb[pl.ds(8 * k, 8)] = tot.astype(BF16)
        rz[myslot] = sb[z16]
        for cp in to_z:
            cp.start()

    for cp in to_z:
        sent.append((holder, cp))
    for i in range(8):
        is_self = jnp.logical_and(holder, myslot == i)

        @pl.when(jnp.logical_not(is_self))
        def _():
            copy(rz.at[i], rz.at[i], zsend, zrecv + i, peer).wait_recv()

    res_cp.wait_recv()
    tiles = []
    for b in range(4):
        attn = (rz[b].astype(F32) + rz[4 + b].astype(F32)).astype(BF16).astype(F32)
        tiles.append(attn)
    attn = jnp.concatenate(tiles, axis=1)
    state = (rt[...].reshape(16, 512) + attn).astype(BF16).astype(F32)
    square = jnp.sum(state * state, axis=1, keepdims=True)
    high = square.astype(BF16).astype(F32)
    low = square - high
    scaled = state * gn[c]
    lane = lax.broadcasted_iota(jnp.int32, (16, 512), 1)
    scaled = jnp.where(lane == OUTCOL, high, jnp.where(lane == OUTCOL + 1, low, scaled))
    g2[c, y, z] = scaled.astype(BF16)
    cps = gather_z(g2)
    st[...] = state.reshape(2, 8, 512)
    st_cp = go(st.at[o], so.at[c], sems(1), peer)
    so[c] = st[c]

    gsem = sems(16)
    gcp = {}

    def gate_up(yd, d):
        left, right = g2[0, yd].reshape(128, 512), g2[1, yd].reshape(128, 512)
        gu = jnp.dot(left, w2[0], preferred_element_type=F32)
        gu = gu + jnp.dot(right, w2[1], preferred_element_type=F32)
        gb[d] = gu.astype(BF16).reshape(NX, 32, 640)
        for e in (1, 3, 2):
            xd = plus(x, e, NX)
            gcp[d, e] = go(gb.at[d, xd], rxg.at[d, e - 1], gsem + d * 4 + e, at(x_=xd))

    gather_rest(g2, cps, gate_up)

    hsem = sems(4)
    other = at(zh_=1 - zh)
    order = (0, 1, 3, 2)
    hcp = {}
    for d in order:
        tot = gb[d, x].astype(F32)
        for e in (1, 3, 2):
            gcp[d, e].wait_recv()
            tot = tot + rxg[d, e - 1].astype(F32)
        sx[d] = tot.astype(BF16)
        hcp[d] = go(sx.at[d], rzh.at[d], hsem + d, other)

    asem = sems(16)
    acp = {}
    for d in order:
        hcp[d].wait_recv()
        gu = sx[d].astype(F32) + rzh[d].astype(F32)
        inv = lax.rsqrt(gu[:, 2 * UNITS : 2 * UNITS + 1] / D + 1e-06)
        gate, up = gu[:, :UNITS] * inv, gu[:, UNITS : 2 * UNITS] * inv
        hid = gate / (1.0 + jnp.exp(-gate)) * up
        hb[d, x, :, :UNITS] = hid.astype(BF16)
        for e in (1, 3, 2):
            acp[d, e] = go(hb.at[d, x], hb.at[d, x], asem + d * 4 + e, at(x_=plus(x, e, NX)))

    dsem = sems(4)
    dcp = {}
    for d in order:
        for e in (1, 3, 2):
            acp[d, e].wait_recv()
        hidden = hb[d].reshape(128, 384)
        there = jnp.dot(hidden, w3[o], preferred_element_type=F32)
        dsend[d] = there.astype(BF16)
        dcp[d] = go(dsend.at[d], drecv.at[d], dsem + d, peer)

    fsem = sems(4)
    fcp = {}
    mine = None
    for d in (1, 3, 2, 0):
        part = jnp.dot(hb[d].reshape(128, 384), w3[c], preferred_element_type=F32)
        dcp[d].wait_recv()
        part = part + drecv[d].astype(F32)
        if d == 0:
            mine = part
        else:
            eb[d - 1] = part.astype(BF16)
            fcp[d] = go(eb.at[d - 1], fr.at[d - 1], fsem + d, at(y_=plus(y, NY - d, NY)))

    st_cp.wait_recv()
    for b in range(8):
        lo = (b // 2) * 128
        stf[:, b * OUTCOL : (b + 1) * OUTCOL] = so[b % 2, :, lo : lo + OUTCOL]

    for d in (1, 3, 2):
        fcp[d].wait_recv()
        mine = mine + fr[d - 1].astype(F32)
    fb[...] = mine.astype(BF16).reshape(NZ, 16, 512)
    osem = sems(8)
    ocp = {}
    for j in (7, 6, 5, 4, 3, 2, 1):
        t = flip(z, j)
        ocp[j] = go(fb.at[t], zr.at[j], osem + j, at(z_=t))
    tot = fb[z].astype(F32)
    for j in range(1, 8):
        ocp[j].wait_recv()
        tot = tot + zr[j].astype(F32)
    osum[...] = tot.reshape(2, 8, 512)
    last = go(osum.at[o], orx.at[c], sems(1), peer)
    orx[c] = osum[c]
    last.wait_recv()
    livew = live[:, :1]
    out[:, :512] = ((stf[:, :512] + orx[0]) * livew).astype(BF16)
    out[:, 512:] = ((stf[:, 512:] + orx[1, :, :384]) * livew).astype(BF16)

    for when, cp in sent:
        if when is None:
            cp.wait_send()
        else:
            pl.when(when)(cp.wait_send)
    assert used[0] <= NSEM


def per_device(query, cache, lengths, counts, value_up, out_proj, residual, norm_gain, gate_w, up_w, down_w):
    vmem, smem = pl.BlockSpec(memory_space=pltpu.VMEM), pl.BlockSpec(memory_space=pltpu.SMEM)
    b, f = lambda *s: pltpu.VMEM(s, BF16), lambda *s: pltpu.VMEM(s, F32)
    return pl.pallas_call(
        kernel,
        out_shape=jax.ShapeDtypeStruct((8, FEAT), BF16),
        in_specs=[vmem, vmem, smem, smem] + [vmem] * 7,
        out_specs=vmem,
        scratch_shapes=[
            f(4, 64, 128), f(2, 8, 512), f(2, 8, 512), b(2, NY, NZ, 16, 512), b(1024, 128),
            b(NY, NZ, 16, 128), b(8, NZ, 16, 128), b(16, 16, 128), b(8, 16, 128),
            f(2, 8, 512), f(2, 8, 512), f(2, 1, 512), f(2, 8, 512), f(2, 8, 512),
            b(2, NY, NZ, 16, 512), b(2, 512, 640), b(NY, NX, 32, 640), b(NY, 3, 32, 640),
            b(NY, 32, 640), b(NY, 32, 640), b(NY, NX, 32, 384), b(2, 384, 512),
            b(NY, 128, 512), b(NY, 128, 512), b(3, 128, 512), b(3, 128, 512),
            b(NZ, 16, 512), b(NZ, 16, 512), f(2, 8, 512), f(2, 8, 512), f(8, FEAT),
            pltpu.SemaphoreType.DMA((NSEM,)), pltpu.SemaphoreType.DMA((NSEM,)),
        ],
        compiler_params=pltpu.CompilerParams(
            collective_id=0, has_side_effects=True, vmem_limit_bytes=48 << 20
        ),
        name="decode_layer",
    )(
        query.reshape(SLOTS, QTOK * HEADS, QK), cache, lengths, counts, value_up, out_proj, residual,
        norm_gain.reshape(1, FEAT), gate_w, up_w, down_w,
    )


def solution(mesh):
    return jax.shard_map(
        per_device,
        mesh=mesh,
        in_specs=(
            P("dp", None, "hd", None), P("dp", None, None), P("dp"), P("dp"), P("hd", None, None), P("hd", "dp"),
            P("dp", "hd"), P("hd"), P("hd", "dp"), P("hd", "dp"), P("dp", "hd"),
        ),
        out_specs=P("dp", "hd"),
        check_vma=False,
    )
```

```python
import functools

import jax
import jax.numpy as jnp
from jax import lax
from jax.experimental import pallas as pl
from jax.experimental.pallas import tpu as pltpu
from jax.sharding import PartitionSpec as P

MESH = pl.DeviceIdType.MESH
F32, BF16 = jnp.float32, jnp.bfloat16
D = 7168
SLOTS, QTOK, HEADS, LAT, QK, POS = 4, 2, 8, 512, 576, 192
NX, NY, NZ, NSEM = 4, 4, 8, 72
OUTCOL, FEAT, UNITS = 112, 896, 288


def flip(value, mask, bits=3):
    out = 0
    for i in range(bits):
        bit = lax.rem(lax.div(value, 1 << i), 2)
        out = out + (1 - bit if (mask >> i) & 1 else bit) * (1 << i)
    return out


def dot_t(a, b):
    return lax.dot_general(a, b, (((1,), (1,)), ((), ())), preferred_element_type=F32)


def kernel(
    query_h, cache_h, lengths_h, counts_h, value_h, proj_h, res_h, gain_h, gate_h, up_h, down_h,
    out,
    query, cache, lengths, counts, value_up, out_proj, residual, norm_gain, gate_w, up_w, down_w, ls,
    lat, hsc, tf, g1, w1, pb, rx, sb, rz, rsp, rt, gn, st, so, g2, w2, gb, rxg, sx, rzh, hb, w3,
    dsend, drecv, eb, fr, fb, zr, osum, orx, stf, acc, ss,
):
    dp, hd = lax.axis_index("dp"), lax.axis_index("hd")
    x, zh = lax.rem(hd, NX), lax.div(hd, NX)
    c, z, y = lax.rem(dp, 2), lax.rem(lax.div(dp, 2), NZ), lax.div(dp, 2 * NZ)
    o = 1 - c

    def at(x_=x, zh_=zh, y_=y, z_=z, c_=c):
        return ((y_ * NZ + z_) * 2 + c_, zh_ * NX + x_)

    def plus(v, d, n):
        return lax.rem(v + d, n)

    used = [0]
    ends = []

    def sems(n):
        first = used[0]
        used[0] += n
        return first

    def copy(src, dst, send, recv, dev):
        return pltpu.make_async_remote_copy(
            src_ref=src, dst_ref=dst, send_sem=ss.at[send], recv_sem=ss.at[recv],
            device_id=dev, device_id_type=MESH,
        )

    def go(src, dst, send, recv, dev):
        copy(src, dst, send, recv, dev).start()

    def arrive(ref, recv):
        copy(ref, ref, recv, recv, peer).wait_recv()

    def sending(ref, when=None):
        send = sems(1)
        ends.append((when, ref, send))
        return send

    barrier = pltpu.get_barrier_semaphore()
    peer = at(c_=o)
    partners = [peer]
    for d in range(1, 16):
        z16 = plus(zh * NZ + z, d, 16)
        partners.append(at(zh_=lax.div(z16, NZ), z_=lax.rem(z16, NZ)))
    for d in range(1, 16):
        partners.append(at(x_=plus(x, d % 4, NX), y_=plus(y, d // 4, NY)))
    for dev in partners:
        pl.semaphore_signal(barrier, inc=1, device_id=dev, device_id_type=MESH)

    loads = {}
    pairs = (
        (query_h, query), (cache_h, cache), (value_h, value_up), (res_h, residual), (gain_h, norm_gain),
        (proj_h, out_proj), (gate_h, gate_w), (up_h, up_w), (down_h, down_w), (lengths_h, lengths), (counts_h, counts),
    )
    for i, (src, dst) in enumerate(pairs):
        loads[i] = pltpu.make_async_copy(src, dst, ls.at[i])
        loads[i].start()

    loads[9].wait()
    row = lax.broadcasted_iota(jnp.int32, (64, POS), 0)
    pos = lax.broadcasted_iota(jnp.int32, (64, POS), 1)
    limit = lax.rem(lax.div(row, HEADS), QTOK) - 1
    for i in range(SLOTS):
        limit = limit + jnp.where(lax.div(row, 16) == i, lengths[i], 0)
    loads[0].wait()
    loads[1].wait()
    sc = [dot_t(query[i], cache[i]) for i in range(SLOTS)]
    sc = jnp.concatenate(sc, axis=0) * F32(192.0**-0.5)
    sc = jnp.where(pos < limit, sc, -1e30)
    ex = jnp.exp(sc - jnp.max(sc, axis=-1, keepdims=True))
    wt = (ex / jnp.sum(ex, axis=-1, keepdims=True)).astype(BF16)
    for i in range(SLOTS):
        la = jnp.dot(wt[16 * i : 16 * i + 16], cache[i, :, :LAT], preferred_element_type=F32)
        la = la.astype(BF16).astype(F32)
        for k in range(4):
            lat[k, pl.ds(i * 16, 16), :] = la[:, k * 128 : (k + 1) * 128]
    loads[2].wait()
    loads[10].wait()
    count = counts[0]
    row8 = lax.broadcasted_iota(jnp.int32, (8, 128), 0)
    live = jnp.where(lax.div(row8, QTOK) < count, F32(1), F32(0))
    for h in range(HEADS):
        lh = [lat[k, pl.ds(h, 8, stride=HEADS), :] for k in range(4)]
        lh = jnp.concatenate(lh, axis=1).astype(BF16)
        hv = jnp.dot(lh, value_up[h], preferred_element_type=F32) * live
        hsc[h // 4, :, (h % 4) * 128 : (h % 4 + 1) * 128] = hv.astype(BF16).astype(F32)

    loads[3].wait()
    loads[4].wait()
    res = residual[...].astype(F32)
    gain = jnp.concatenate([norm_gain[i : i + 1, :] for i in range(7)], axis=1)
    rsp[...] = jnp.zeros_like(rsp)
    gn[...] = jnp.zeros_like(gn)
    for b in range(8):
        lo = (b // 2) * 128
        rsp[b % 2, :, lo : lo + OUTCOL] = res[:, b * OUTCOL : (b + 1) * OUTCOL]
        gn[b % 2, :, lo : lo + OUTCOL] = gain[:, b * OUTCOL : (b + 1) * OUTCOL]

    w1[...] = jnp.zeros_like(w1)
    loads[5].wait()
    w1[:OUTCOL, :] = out_proj[...]

    pl.semaphore_wait(barrier, len(partners))

    heads_in, res_in = sems(1), sems(1)
    go(hsc.at[o], tf.at[c], sending(hsc.at[0]), heads_in, peer)
    go(rsp.at[o], rt.at[c], sending(rsp.at[0]), res_in, peer)
    tf[c] = hsc[c]
    rt[c] = rsp[c]
    arrive(tf.at[c], heads_in)
    g1[c, y, z] = tf[...].reshape(16, 512).astype(BF16)

    def gather_z(g):
        send, recv = sending(g.at[0, 0, pl.ds(0, 7)]), sems(2)
        for j in (7, 6, 5, 4, 3, 2, 1):
            go(g.at[c, y, z], g.at[c, y, z], send, recv + j // 4, at(z_=flip(z, j)))
        return recv

    def gather_y(g, zrecv, consume):
        ysend, csend, yrecv, crecv = sending(g.at[0, pl.ds(0, 3)]), sending(g.at[0]), sems(8), sems(4)
        near = lax.div(z, 4) * 4
        base = (near, 4 - near)
        for gi in range(2):
            arrive(g.at[c, y, pl.ds(base[gi], 3 + gi)], zrecv + gi)
            part = g.at[c, y, pl.ds(base[gi], 4)]
            for d in (2, 1, 3):
                go(part, part, ysend, yrecv + gi * 4 + d, at(y_=plus(y, d, NY)))
            go(part, part, csend, crecv, peer)

        def forward(d):
            yd = plus(y, NY - d, NY)
            for gi in range(2):
                part = g.at[c, yd, pl.ds(base[gi], 4)]
                arrive(part, yrecv + gi * 4 + d)
                go(part, part, csend, crecv + d, peer)

        def take(d):
            yd = plus(y, NY - d, NY)
            arrive(g.at[o, yd], crecv + d)
            consume(yd, d)

        return forward, take

    cps = gather_z(g1)

    w2[...] = jnp.zeros_like(w2)
    loads[6].wait()
    loads[7].wait()
    for b in range(8):
        lo = (b // 2) * 128
        w2[b % 2, :UNITS, lo : lo + OUTCOL] = gate_w[:, b * OUTCOL : (b + 1) * OUTCOL]
        w2[b % 2, UNITS : 2 * UNITS, lo : lo + OUTCOL] = up_w[:, b * OUTCOL : (b + 1) * OUTCOL]
    r_ = lax.broadcasted_iota(jnp.int32, (16, 128), 0)
    c_ = lax.broadcasted_iota(jnp.int32, (16, 128), 1)
    ones = jnp.where((r_ == 0) & (c_ >= OUTCOL) & (c_ < OUTCOL + 2), F32(1), F32(0)).astype(BF16)
    for k in range(2):
        w2[k, 2 * UNITS : 2 * UNITS + 16, :128] = ones
    hb[...] = jnp.zeros_like(hb)

    xt = lax.rem(y, 2) * 2 + lax.div(z, 4)
    here = x == xt
    slot = lax.div(y, 2) * 4 + x
    psend, pself, precv = sending(pb.at[pl.ds(0, 3)]), sending(pb.at[0], jnp.logical_not(here)), sems(2)

    def out_projection(yd, d):
        left, right = g1[0, yd].reshape(128, 512), g1[1, yd].reshape(128, 512)
        pv = dot_t(left, w1[:, :512]) + dot_t(right, w1[:, 512:])
        pb[yd] = pv.astype(BF16).reshape(NZ, 16, 128)
        cp = copy(pb.at[yd], rx.at[slot], psend if d else pself, precv + lax.div(y, 2), at(x_=xt, y_=yd))
        if d:
            cp.start()
        else:
            pl.when(jnp.logical_not(here))(cp.start)

            @pl.when(here)
            def _():
                rx[slot] = pb[yd]

    forward, take = gather_y(g1, cps, out_projection)
    take(0)
    forward(1)
    forward(3)
    take(1)
    forward(2)
    take(3)
    take(2)

    holder = lax.rem(x, 2) == lax.div(z, 4)
    own = jnp.logical_and(holder, lax.rem(y, 2) == lax.div(x, 2))
    zsend, zrecv = sending(sb.at[pl.ds(0, 15)], holder), sems(1)
    z16 = zh * NZ + z
    myslot = zh * 4 + lax.rem(z, 4)

    for k in (1 - zh, zh):

        @pl.when(holder)
        def _():
            is_self = jnp.logical_and(own, lax.div(y, 2) == k)
            pl.when(is_self)(lambda: arrive(rx.at[pl.ds(0, 3)], precv + k))
            pl.when(jnp.logical_not(is_self))(lambda: arrive(rx.at[pl.ds(0, 4)], precv + k))
            tot = rx[4 * k].astype(F32) + rx[4 * k + 1].astype(F32)
            tot = tot + rx[4 * k + 2].astype(F32) + rx[4 * k + 3].astype(F32)
            sb[pl.ds(8 * k, 8)] = tot.astype(BF16)
            for d in (4, 3, 5, 2, 6, 1, 7, 0):
                zd = plus(z, d, NZ)
                cp = copy(sb.at[8 * k + zd], rz.at[myslot], zsend, zrecv, at(zh_=k, z_=zd))
                if d:
                    cp.start()
                else:
                    pl.when(k != zh)(cp.start)

    @pl.when(holder)
    def _():
        rz[myslot] = sb[z16]

    w3[...] = jnp.zeros_like(w3)
    loads[8].wait()
    w3[0, :UNITS, :] = down_w[:, :512]
    w3[1, :UNITS, :384] = down_w[:, 512:]
    pl.when(holder)(lambda: arrive(rz.at[pl.ds(0, 7)], zrecv))
    pl.when(jnp.logical_not(holder))(lambda: arrive(rz, zrecv))

    arrive(rt.at[c], res_in)
    tiles = []
    for b in range(4):
        attn = (rz[b].astype(F32) + rz[4 + b].astype(F32)).astype(BF16).astype(F32)
        tiles.append(attn)
    attn = jnp.concatenate(tiles, axis=1)
    state = (rt[...].reshape(16, 512) + attn).astype(BF16).astype(F32)
    square = jnp.sum(state * state, axis=1, keepdims=True)
    high = square.astype(BF16).astype(F32)
    low = square - high
    scaled = state * gn[c]
    lane = lax.broadcasted_iota(jnp.int32, (16, 512), 1)
    scaled = jnp.where(lane == OUTCOL, high, jnp.where(lane == OUTCOL + 1, low, scaled))
    g2[c, y, z] = scaled.astype(BF16)
    cps = gather_z(g2)
    st[...] = state.reshape(2, 8, 512)
    st_in = sems(1)
    go(st.at[o], so.at[c], sending(st.at[0]), st_in, peer)
    so[c] = st[c]

    gsend, grecv = sending(gb.at[pl.ds(0, 3)]), sems(4)

    def gate_up(yd, d):
        left, right = g2[0, yd].reshape(128, 512), g2[1, yd].reshape(128, 512)
        gu = dot_t(left, w2[0]) + dot_t(right, w2[1])
        gb[d] = gu.astype(BF16).reshape(NX, 32, 640)
        for e in (1, 3, 2):
            xd = plus(x, e, NX)
            go(gb.at[d, xd], rxg.at[d, e - 1], gsend, grecv + d, at(x_=xd))

    hsend, hrecv = sending(sx), sems(4)
    other = at(zh_=1 - zh)

    def sum_x(d):
        tot = gb[d, x].astype(F32)
        arrive(rxg.at[d], grecv + d)
        for e in (1, 3, 2):
            tot = tot + rxg[d, e - 1].astype(F32)
        sx[d] = tot.astype(BF16)
        go(sx.at[d], rzh.at[d], hsend, hrecv + d, other)

    asend, arecv = sending(hb.at[pl.ds(0, 3)]), sems(4)

    def hidden_units(d):
        arrive(rzh.at[d], hrecv + d)
        gu = sx[d].astype(F32) + rzh[d].astype(F32)
        inv = lax.rsqrt(gu[:, 2 * UNITS : 2 * UNITS + 1] / D + 1e-06)
        gate, up = gu[:, :UNITS] * inv, gu[:, UNITS : 2 * UNITS] * inv
        hid = gate / (1.0 + jnp.exp(-gate)) * up
        hb[d, x, :, :UNITS] = hid.astype(BF16)
        for e in (1, 3, 2):
            go(hb.at[d, x], hb.at[d, x], asend, arecv + d, at(x_=plus(x, e, NX)))

    dout, din = sending(dsend), sems(4)

    def down_there(d):
        arrive(hb.at[d, pl.ds(0, 3)], arecv + d)
        there = jnp.dot(hb[d].reshape(128, 384), w3[o], preferred_element_type=F32)
        dsend[d] = there.astype(BF16)
        go(dsend.at[d], drecv.at[d], dout, din + d, peer)

    fsend, frecv = sending(eb), sems(1)

    def down_here(d):
        part = jnp.dot(hb[d].reshape(128, 384), w3[c], preferred_element_type=F32)
        arrive(drecv.at[d], din + d)
        part = part + drecv[d].astype(F32)
        if d == 0:
            acc[...] = part.reshape(NZ, 16, 512)
        else:
            eb[d - 1] = part.astype(BF16).reshape(NZ, 16, 512)
            go(eb.at[d - 1], fr.at[d - 1], fsend, frecv, at(y_=plus(y, NY - d, NY)))

    forward, take = gather_y(g2, cps, gate_up)
    take(0)
    forward(1)
    forward(3)
    take(1)
    sum_x(0)
    forward(2)
    take(3)
    take(2)
    sum_x(1)
    sum_x(3)
    sum_x(2)
    hidden_units(0)
    down_there(0)
    hidden_units(1)
    hidden_units(3)
    down_here(0)
    hidden_units(2)
    down_there(1)
    down_there(3)
    down_here(1)
    down_here(3)
    down_there(2)
    down_here(2)

    arrive(so.at[c], st_in)
    for b in range(8):
        lo = (b // 2) * 128
        stf[:, b * OUTCOL : (b + 1) * OUTCOL] = so[b % 2, :, lo : lo + OUTCOL]

    arrive(fr, frecv)
    oout, oin = sending(fb.at[pl.ds(0, 7)]), sems(1)

    def sum_y(t):
        return acc[t] + fr[0, t].astype(F32) + fr[1, t].astype(F32) + fr[2, t].astype(F32)

    for j in (7, 6, 5, 4, 3, 2, 1):
        t = flip(z, j)
        fb[t] = sum_y(t).astype(BF16)
        go(fb.at[t], zr.at[j - 1], oout, oin, at(z_=t))
    tot = sum_y(z)
    arrive(zr, oin)
    for j in range(7):
        tot = tot + zr[j].astype(F32)
    osum[...] = tot.reshape(2, 8, 512)
    last = sems(1)
    go(osum.at[o], orx.at[c], sending(osum.at[0]), last, peer)
    orx[c] = osum[c]
    arrive(orx.at[c], last)
    livew = live[:, :1]
    out[:, :512] = ((stf[:, :512] + orx[0]) * livew).astype(BF16)
    out[:, 512:] = ((stf[:, 512:] + orx[1, :, :384]) * livew).astype(BF16)

    for when, ref, send in ends:
        if when is None:
            copy(ref, ref, send, send, peer).wait_send()
        else:
            pl.when(when)(lambda ref=ref, send=send: copy(ref, ref, send, send, peer).wait_send())
    assert used[0] == NSEM, used


def per_device(query, cache, lengths, counts, value_up, out_proj, residual, norm_gain, gate_w, up_w, down_w):
    hbm = pl.BlockSpec(memory_space=pltpu.HBM)
    vmem = pl.BlockSpec(memory_space=pltpu.VMEM)
    b, f = lambda *s: pltpu.VMEM(s, BF16), lambda *s: pltpu.VMEM(s, F32)
    return pl.pallas_call(
        kernel,
        out_shape=jax.ShapeDtypeStruct((8, FEAT), BF16),
        in_specs=[hbm] * 11,
        out_specs=vmem,
        scratch_shapes=[
            b(SLOTS, 16, QK), b(SLOTS, POS, QK), pltpu.SMEM((4,), jnp.int32), pltpu.SMEM((1,), jnp.int32), b(HEADS, LAT, 128), b(OUTCOL, 1024), b(8, FEAT), f(7, 128),
            b(UNITS, FEAT), b(UNITS, FEAT), b(UNITS, FEAT), pltpu.SemaphoreType.DMA((11,)),
            f(4, 64, 128), f(2, 8, 512), f(2, 8, 512), b(2, NY, NZ, 16, 512), b(128, 1024),
            b(NY, NZ, 16, 128), b(8, NZ, 16, 128), b(16, 16, 128), b(8, 16, 128),
            f(2, 8, 512), f(2, 8, 512), f(2, 1, 512), f(2, 8, 512), f(2, 8, 512),
            b(2, NY, NZ, 16, 512), b(2, 640, 512), b(NY, NX, 32, 640), b(NY, 3, 32, 640),
            b(NY, 32, 640), b(NY, 32, 640), b(NY, NX, 32, 384), b(2, 384, 512),
            b(NY, 128, 512), b(NY, 128, 512), b(3, NZ, 16, 512), b(3, NZ, 16, 512),
            b(NZ, 16, 512), b(7, 16, 512), f(2, 8, 512), f(2, 8, 512), f(8, FEAT), f(NZ, 16, 512),
            pltpu.SemaphoreType.DMA((NSEM,)),
        ],
        compiler_params=pltpu.CompilerParams(
            collective_id=0, has_side_effects=True, vmem_limit_bytes=60 << 20
        ),
        name="decode_layer",
    )(
        query.reshape(SLOTS, QTOK * HEADS, QK), cache, lengths, counts, value_up, out_proj.T, residual,
        norm_gain.reshape(7, 128), gate_w.T, up_w.T, down_w,
    )


def solution(mesh):
    return jax.shard_map(
        per_device,
        mesh=mesh,
        in_specs=(
            P("dp", None, "hd", None), P("dp", None, None), P("dp"), P("dp"), P("hd", None, None), P("hd", "dp"),
            P("dp", "hd"), P("hd"), P("hd", "dp"), P("hd", "dp"), P("dp", "hd"),
        ),
        out_specs=P("dp", "hd"),
        check_vma=False,
    )
```

```python
import functools

import jax
import jax.numpy as jnp
from jax import lax
from jax.experimental import pallas as pl
from jax.experimental.pallas import tpu as pltpu
from jax.sharding import PartitionSpec as P

MESH = pl.DeviceIdType.MESH
F32, BF16 = jnp.float32, jnp.bfloat16
D = 7168
SLOTS, QTOK, HEADS, LAT, QK, POS = 4, 2, 8, 512, 576, 192
NX, NY, NZ, NSEM = 4, 4, 8, 72
OUTCOL, FEAT, UNITS = 112, 896, 288


def flip(value, mask, bits=3):
    out = 0
    for i in range(bits):
        bit = lax.rem(lax.div(value, 1 << i), 2)
        out = out + (1 - bit if (mask >> i) & 1 else bit) * (1 << i)
    return out


def dot_t(a, b):
    return lax.dot_general(a, b, (((1,), (1,)), ((), ())), preferred_element_type=F32)


def kernel(
    query_h, cache_h, lengths_h, counts_h, value_h, proj_h, res_h, gain_h, gate_h, up_h, down_h,
    out,
    query, cache, lengths, counts, value_up, out_proj, residual, norm_gain, gate_w, up_w, down_w, ls,
    lat, hsc, g1, w1, pb, rx, sb, rz, rsp, rt, gn, st, so, g2, w2, gb, rxg, sx, rzh, hb, w3, w3x,
    eb, fr, fb, zr, stf, acc, ss,
):
    dp, hd = lax.axis_index("dp"), lax.axis_index("hd")
    x, zh = lax.rem(hd, NX), lax.div(hd, NX)
    c, z, y = lax.rem(dp, 2), lax.rem(lax.div(dp, 2), NZ), lax.div(dp, 2 * NZ)
    o = 1 - c

    def at(x_=x, zh_=zh, y_=y, z_=z, c_=c):
        return ((y_ * NZ + z_) * 2 + c_, zh_ * NX + x_)

    def plus(v, d, n):
        return lax.rem(v + d, n)

    used = [0]
    ends = []

    def sems(n):
        first = used[0]
        used[0] += n
        return first

    def copy(src, dst, send, recv, dev):
        return pltpu.make_async_remote_copy(
            src_ref=src, dst_ref=dst, send_sem=ss.at[send], recv_sem=ss.at[recv],
            device_id=dev, device_id_type=MESH,
        )

    def go(src, dst, send, recv, dev):
        copy(src, dst, send, recv, dev).start()

    def arrive(ref, recv):
        copy(ref, ref, recv, recv, peer).wait_recv()

    def sending(ref, when=None):
        send = sems(1)
        ends.append((when, ref, send))
        return send

    barrier = pltpu.get_barrier_semaphore()
    peer = at(c_=o)
    barrier = pltpu.get_barrier_semaphore()
    partners = []
    for d in (8, 7, 9, 6, 10, 5, 11, 4, 12, 3, 13, 2, 14, 1, 15):
        z16 = plus(zh * NZ + z, d, 16)
        partners.append(at(zh_=lax.div(z16, NZ), z_=lax.rem(z16, NZ)))
    for d in range(15, 0, -1):
        partners.append(at(x_=plus(x, d % 4, NX), y_=plus(y, d // 4, NY)))
    partners.append(peer)
    partners += [at(x_=plus(x, d, NX), c_=o) for d in (1, 2, 3)]
    for dev in partners[:15]:
        pl.semaphore_signal(barrier, inc=1, device_id=dev, device_id_type=MESH)

    loads = {}
    pairs = (
        (query_h, query), (cache_h, cache), (value_h, value_up), (res_h, residual), (gain_h, norm_gain),
        (proj_h, out_proj), (gate_h, gate_w), (up_h, up_w), (down_h, down_w), (lengths_h, lengths), (counts_h, counts),
    )
    for i, (src, dst) in enumerate(pairs):
        loads[i] = pltpu.make_async_copy(src, dst, ls.at[i])
        loads[i].start()
    for dev in partners[15:]:
        pl.semaphore_signal(barrier, inc=1, device_id=dev, device_id_type=MESH)

    loads[9].wait()
    row = lax.broadcasted_iota(jnp.int32, (64, POS), 0)
    pos = lax.broadcasted_iota(jnp.int32, (64, POS), 1)
    limit = lax.rem(lax.div(row, HEADS), QTOK) - 1
    for i in range(SLOTS):
        limit = limit + jnp.where(lax.div(row, 16) == i, lengths[i], 0)
    loads[0].wait()
    loads[1].wait()
    sc = [dot_t(query[i], cache[i]) for i in range(SLOTS)]
    sc = jnp.concatenate(sc, axis=0) * F32(192.0**-0.5)
    sc = jnp.where(pos < limit, sc, -1e30)
    ex = jnp.exp(sc - jnp.max(sc, axis=-1, keepdims=True))
    wt = (ex / jnp.sum(ex, axis=-1, keepdims=True)).astype(BF16)
    for i in range(SLOTS):
        la = jnp.dot(wt[16 * i : 16 * i + 16], cache[i, :, :LAT], preferred_element_type=F32)
        la = la.astype(BF16).astype(F32)
        for k in range(4):
            lat[k, pl.ds(i * 16, 16), :] = la[:, k * 128 : (k + 1) * 128]
    loads[2].wait()
    loads[10].wait()
    count = counts[0, 0]
    row8 = lax.broadcasted_iota(jnp.int32, (8, 128), 0)
    live = jnp.where(lax.div(row8, QTOK) < count, F32(1), F32(0))
    for h in range(HEADS):
        lh = [lat[k, pl.ds(h, 8, stride=HEADS), :] for k in range(4)]
        lh = jnp.concatenate(lh, axis=1).astype(BF16)
        hv = jnp.dot(lh, value_up[h], preferred_element_type=F32) * live
        hsc[h // 4, :, (h % 4) * 128 : (h % 4 + 1) * 128] = hv.astype(BF16).astype(F32)

    loads[3].wait()
    loads[4].wait()
    res = residual[...].astype(F32)
    gain = jnp.concatenate([norm_gain[i : i + 1, :] for i in range(7)], axis=1)
    rsp[...] = jnp.zeros_like(rsp)
    gn[...] = jnp.zeros_like(gn)
    for b in range(8):
        lo = (b // 2) * 128
        rsp[b % 2, :, lo : lo + OUTCOL] = res[:, b * OUTCOL : (b + 1) * OUTCOL]
        gn[b % 2, :, lo : lo + OUTCOL] = gain[:, b * OUTCOL : (b + 1) * OUTCOL]

    w1[...] = jnp.zeros_like(w1)
    loads[5].wait()
    w1[:OUTCOL, :] = out_proj[:, :512]
    w1[128 : 128 + OUTCOL, :] = out_proj[:, 512:]

    pl.semaphore_wait(barrier, len(partners))

    g1[c, y, z] = hsc[...].reshape(16, 512).astype(BF16)

    def gather_z(g):
        send, recv = sending(g.at[0, 0, pl.ds(0, 7)]), sems(3)
        for j in (7, 6, 5, 4, 3, 2, 1):
            go(g.at[c, y, z], g.at[c, y, z], send, recv + max(j // 2 - 1, 0), at(z_=flip(z, j)))
        return recv

    def gather_y(g, zrecv, consume, finish):
        ysend, csend, yrecv, crecv = sending(g.at[0, pl.ds(0, 3)]), sending(g.at[0]), sems(9), sems(4)
        parts = ((lax.div(z, 4) * 4, 4), (lax.div(flip(z, 4), 2) * 2, 2), (lax.div(flip(z, 6), 2) * 2, 2))
        for gi, (base, n) in enumerate(parts):
            arrive(g.at[c, y, pl.ds(base, n if gi else 3)], zrecv + gi)
            part = g.at[c, y, pl.ds(base, n)]
            for d in (2, 1, 3):
                go(part, part, ysend, yrecv + gi * 3 + d - 1, at(y_=plus(y, d, NY)))
            go(part, part, csend, crecv, peer)

        def forward(d):
            yd = plus(y, NY - d, NY)
            for gi, (base, n) in enumerate(parts):
                part = g.at[c, yd, pl.ds(base, n)]
                arrive(part, yrecv + gi * 3 + d - 1)
                go(part, part, csend, crecv + d, peer)

        def take(d):
            yd = plus(y, NY - d, NY)
            first = consume(g[c, yd].reshape(128, 512), c)
            arrive(g.at[o, yd], crecv + d)
            finish(first, consume(g[o, yd].reshape(128, 512), o), yd, d)

        return forward, take

    zin = gather_z(g1)
    res_in = sems(1)
    go(rsp.at[o], rt.at[c], sending(rsp.at[0]), res_in, peer)
    rt[c] = rsp[c]

    w2[...] = jnp.zeros_like(w2)
    loads[6].wait()
    loads[7].wait()
    for b in range(8):
        lo = (b // 2) * 128
        w2[b % 2, :UNITS, lo : lo + OUTCOL] = gate_w[:, b * OUTCOL : (b + 1) * OUTCOL]
        w2[b % 2, UNITS : 2 * UNITS, lo : lo + OUTCOL] = up_w[:, b * OUTCOL : (b + 1) * OUTCOL]
    r_ = lax.broadcasted_iota(jnp.int32, (16, 128), 0)
    c_ = lax.broadcasted_iota(jnp.int32, (16, 128), 1)
    ones = jnp.where((r_ == 0) & (c_ >= OUTCOL) & (c_ < OUTCOL + 2), F32(1), F32(0)).astype(BF16)
    for k in range(2):
        w2[k, 2 * UNITS : 2 * UNITS + 16, :128] = ones
    mine = c * NX + x
    for d in range(NY):
        hb[d, mine, :, 256:] = jnp.zeros((32, 128), BF16)

    xt = lax.rem(y, 2) * 2 + lax.div(z, 4)
    here = x == xt
    slot = lax.div(y, 2) * 4 + x
    psend, pself, precv = sending(pb.at[pl.ds(0, 3)]), sending(pb.at[0], jnp.logical_not(here)), sems(2)

    def project(block, k):
        both = dot_t(block, w1[...]).reshape(NZ, 16, 256)
        return both[:, :8, :128] + both[:, 8:, 128:]

    def out_projection(first, second, yd, d):
        pv = jnp.stack([jnp.where(c == 0, first, second), jnp.where(c == 0, second, first)], axis=1)
        pb[yd] = pv.reshape(NZ, 16, 128).astype(BF16)
        cp = copy(pb.at[yd], rx.at[slot], psend if d else pself, precv + lax.div(y, 2), at(x_=xt, y_=yd))
        if d:
            cp.start()
        else:
            pl.when(jnp.logical_not(here))(cp.start)

            @pl.when(here)
            def _():
                rx[slot] = pb[yd]

    forward, take = gather_y(g1, zin, project, out_projection)
    take(0)
    forward(1)
    forward(3)
    take(1)
    forward(2)
    take(3)
    take(2)

    holder = lax.rem(x, 2) == lax.div(z, 4)
    own = jnp.logical_and(holder, lax.rem(y, 2) == lax.div(x, 2))
    zsend, zrecv = sending(sb.at[pl.ds(0, 15)], holder), sems(1)
    z16 = zh * NZ + z
    myslot = zh * 4 + lax.rem(z, 4)

    for k in (1 - zh, zh):

        @pl.when(holder)
        def _():
            is_self = jnp.logical_and(own, lax.div(y, 2) == k)
            pl.when(is_self)(lambda: arrive(rx.at[pl.ds(0, 3)], precv + k))
            pl.when(jnp.logical_not(is_self))(lambda: arrive(rx.at[pl.ds(0, 4)], precv + k))
            tot = rx[4 * k].astype(F32) + rx[4 * k + 1].astype(F32)
            tot = tot + rx[4 * k + 2].astype(F32) + rx[4 * k + 3].astype(F32)
            sb[pl.ds(8 * k, 8)] = tot.astype(BF16)
            for d in (4, 3, 5, 2, 6, 1, 7, 0):
                zd = plus(z, d, NZ)
                cp = copy(sb.at[8 * k + zd], rz.at[myslot], zsend, zrecv, at(zh_=k, z_=zd))
                if d:
                    cp.start()
                else:
                    pl.when(k != zh)(cp.start)

    @pl.when(holder)
    def _():
        rz[myslot] = sb[z16]

    w3[...] = jnp.zeros_like(w3)
    loads[8].wait()
    w3[0, :UNITS, :] = down_w[:, :512]
    w3[1, :UNITS, :384] = down_w[:, 512:]
    w3_in = sems(1)
    go(w3.at[o], w3x, sending(w3x), w3_in, peer)
    pl.when(holder)(lambda: arrive(rz.at[pl.ds(0, 7)], zrecv))
    pl.when(jnp.logical_not(holder))(lambda: arrive(rz, zrecv))

    arrive(rt.at[c], res_in)
    tiles = []
    for b in range(4):
        attn = (rz[b].astype(F32) + rz[4 + b].astype(F32)).astype(BF16).astype(F32)
        tiles.append(attn)
    attn = jnp.concatenate(tiles, axis=1)
    state = (rt[...].reshape(16, 512) + attn).astype(BF16).astype(F32)
    square = jnp.sum(state * state, axis=1, keepdims=True)
    high = square.astype(BF16).astype(F32)
    low = square - high
    scaled = state * gn[c]
    lane = lax.broadcasted_iota(jnp.int32, (16, 512), 1)
    scaled = jnp.where(lane == OUTCOL, high, jnp.where(lane == OUTCOL + 1, low, scaled))
    g2[c, y, z] = scaled.astype(BF16)
    zin = gather_z(g2)
    st[...] = state.reshape(2, 8, 512)
    st_in = sems(1)
    go(st.at[o], so.at[c], sending(st.at[0]), st_in, peer)
    so[c] = st[c]

    gsend, grecv = sending(gb.at[pl.ds(0, 3)]), sems(4)

    def gate_up_half(block, k):
        return dot_t(block, w2[k])

    def gate_up(first, second, yd, d):
        gb[d] = (first + second).astype(BF16).reshape(NX, 32, 640)
        for e in (1, 3, 2):
            xd = plus(x, e, NX)
            go(gb.at[d, xd], rxg.at[d, e - 1], gsend, grecv + d, at(x_=xd))

    hsend, hrecv = sending(sx), sems(4)
    other = at(zh_=1 - zh)

    def sum_x(d):
        tot = gb[d, x].astype(F32)
        arrive(rxg.at[d], grecv + d)
        for e in (1, 3, 2):
            tot = tot + rxg[d, e - 1].astype(F32)
        sx[d] = tot.astype(BF16)
        go(sx.at[d], rzh.at[d], hsend, hrecv + d, other)

    asend, arecv = [sending(hb.at[0, pl.ds(0, 7)]) for _ in range(NY)], sems(4)

    def hidden_units(d):
        arrive(rzh.at[d], hrecv + d)
        gu = sx[d].astype(F32) + rzh[d].astype(F32)
        inv = lax.rsqrt(gu[:, 2 * UNITS : 2 * UNITS + 1] / D + 1e-06)
        gate, up = gu[:, :UNITS] * inv, gu[:, UNITS : 2 * UNITS] * inv
        hid = gate / (1.0 + jnp.exp(-gate)) * up
        hb[d, mine, :, :UNITS] = hid.astype(BF16)
        for e in (2, 1, 3, 0):
            for dev in (at(x_=plus(x, e, NX)), at(x_=plus(x, e, NX), c_=o))[e == 0 :]:
                go(hb.at[d, mine], hb.at[d, mine], asend[d], arecv + d, dev)

    fsend, frecv = sending(eb), sems(1)

    def down(d):
        arrive(hb.at[d, pl.ds(0, 7)], arecv + d)
        own_, other_ = hb[d, pl.ds(c * NX, NX)].reshape(128, 384), hb[d, pl.ds(o * NX, NX)].reshape(128, 384)
        part = jnp.dot(own_, w3[c], preferred_element_type=F32)
        part = part + jnp.dot(other_, w3x[...], preferred_element_type=F32)
        if d == 0:
            acc[...] = part.reshape(NZ, 16, 512)
        else:
            eb[d - 1] = part.astype(BF16).reshape(NZ, 16, 512)
            go(eb.at[d - 1], fr.at[d - 1], fsend, frecv, at(y_=plus(y, NY - d, NY)))

    forward, take = gather_y(g2, zin, gate_up_half, gate_up)
    take(0)
    forward(1)
    forward(3)
    take(1)
    sum_x(0)
    forward(2)
    take(3)
    take(2)
    sum_x(1)
    sum_x(3)
    sum_x(2)
    hidden_units(0)
    arrive(w3x, w3_in)
    hidden_units(1)
    hidden_units(3)
    down(0)
    hidden_units(2)
    down(1)
    down(3)
    down(2)

    arrive(so.at[c], st_in)
    for b in range(8):
        lo = (b // 2) * 128
        stf[:, b * OUTCOL : (b + 1) * OUTCOL] = so[b % 2, :, lo : lo + OUTCOL]

    arrive(fr, frecv)
    oout, oin = sending(fb.at[pl.ds(0, 15)]), sems(1)

    def sum_y(t):
        return acc[t] + fr[0, t].astype(F32) + fr[1, t].astype(F32) + fr[2, t].astype(F32)

    for j in (7, 6, 5, 4, 3, 2, 1, 0):
        t = flip(z, j)
        tot = sum_y(t).astype(BF16).astype(F32)
        for k in range(2):
            rows = tot[8 * k : 8 * k + 8]
            fb[2 * j + k] = jnp.concatenate([rows[:, :256], rows[:, 256:]], axis=0).astype(BF16)
        if j:
            for k in range(2):
                go(fb.at[2 * j + k], zr.at[2 * j + c], oout, oin, at(z_=t, c_=k))
    go(fb.at[o], zr.at[c], oout, oin, peer)
    zr[c] = fb[c]
    arrive(zr.at[pl.ds(0, 15)], oin)
    cols = []
    for k in range(2):
        tot = zr[k].astype(F32)
        for j in range(1, 8):
            tot = tot + zr[2 * j + k].astype(F32)
        cols.append(jnp.concatenate([tot[:8], tot[8:]], axis=1))
    livew = live[:, :1]
    out[:, :512] = ((stf[:, :512] + cols[0]) * livew).astype(BF16)
    out[:, 512:] = ((stf[:, 512:] + cols[1][:, :384]) * livew).astype(BF16)

    for when, ref, send in ends:
        if when is None:
            copy(ref, ref, send, send, peer).wait_send()
        else:
            pl.when(when)(lambda ref=ref, send=send: copy(ref, ref, send, send, peer).wait_send())
    assert used[0] == NSEM, used


def per_device(query, cache, lengths, counts, value_up, out_proj, residual, norm_gain, gate_w, up_w, down_w):
    hbm = pl.BlockSpec(memory_space=pltpu.HBM)
    vmem = pl.BlockSpec(memory_space=pltpu.VMEM)
    b, f = lambda *s: pltpu.VMEM(s, BF16), lambda *s: pltpu.VMEM(s, F32)
    return pl.pallas_call(
        kernel,
        out_shape=jax.ShapeDtypeStruct((8, FEAT), BF16),
        in_specs=[hbm] * 11,
        out_specs=vmem,
        scratch_shapes=[
            b(SLOTS, 16, QK), b(SLOTS, POS, QK), pltpu.SMEM((4,), jnp.int32), pltpu.SMEM((1, 1), jnp.int32), b(HEADS, LAT, 128), b(OUTCOL, 1024), b(8, FEAT), f(7, 128),
            b(UNITS, FEAT), b(UNITS, FEAT), b(UNITS, FEAT), pltpu.SemaphoreType.DMA((11,)),
            f(4, 64, 128), f(2, 8, 512), b(2, NY, NZ, 16, 512), b(256, 512),
            b(NY, NZ, 16, 128), b(8, NZ, 16, 128), b(16, 16, 128), b(8, 16, 128),
            f(2, 8, 512), f(2, 8, 512), f(2, 1, 512), f(2, 8, 512), f(2, 8, 512),
            b(2, NY, NZ, 16, 512), b(2, 640, 512), b(NY, NX, 32, 640), b(NY, 3, 32, 640),
            b(NY, 32, 640), b(NY, 32, 640), b(NY, 2 * NX, 32, 384), b(2, 384, 512), b(384, 512),
            b(3, NZ, 16, 512), b(3, NZ, 16, 512),
            b(16, 16, 256), b(16, 16, 256), f(8, FEAT), f(NZ, 16, 512),
            pltpu.SemaphoreType.DMA((NSEM,)),
        ],
        compiler_params=pltpu.CompilerParams(
            collective_id=0, has_side_effects=True, vmem_limit_bytes=60 << 20
        ),
        name="decode_layer",
    )(
        query.reshape(SLOTS, QTOK * HEADS, QK), cache, lengths, counts.reshape(1, 1), value_up, out_proj.T, residual,
        norm_gain.reshape(7, 128), gate_w.T, up_w.T, down_w,
    )


def solution(mesh):
    return jax.shard_map(
        per_device,
        mesh=mesh,
        in_specs=(
            P("dp", None, "hd", None), P("dp", None, None), P("dp"), P("dp"), P("hd", None, None), P("hd", "dp"),
            P("dp", "hd"), P("hd"), P("hd", "dp"), P("hd", "dp"), P("dp", "hd"),
        ),
        out_specs=P("dp", "hd"),
        check_vma=False,
    )
```

```python
import functools

import jax
import jax.numpy as jnp
from jax import lax
from jax.experimental import pallas as pl
from jax.experimental.pallas import tpu as pltpu
from jax.sharding import PartitionSpec as P

MESH = pl.DeviceIdType.MESH
F32, BF16 = jnp.float32, jnp.bfloat16
D = 7168
SLOTS, QTOK, HEADS, LAT, QK, POS = 4, 2, 8, 512, 576, 192
NX, NY, NZ, NSEM = 4, 4, 8, 72
OUTCOL, FEAT, UNITS = 112, 896, 288


def flip(value, mask, bits=3):
    out = 0
    for i in range(bits):
        bit = lax.rem(lax.div(value, 1 << i), 2)
        out = out + (1 - bit if (mask >> i) & 1 else bit) * (1 << i)
    return out


def apart(a, b, unit):
    p, q = lax.rem(lax.div(a, unit), 2), lax.rem(lax.div(b, unit), 2)
    return p + q - 2 * p * q


def dot_t(a, b):
    return lax.dot_general(a, b, (((1,), (1,)), ((), ())), preferred_element_type=F32)


def kernel(
    query_h, cache_h, lengths_h, counts_h, value_h, proj_h, res_h, gain_h, gate_h, up_h, down_h,
    out,
    query, cache, lengths, counts, value_up, out_proj, residual, norm_gain, gate_w, up_w, down_w, ls,
    lat, hsc, g1, w1, pb, rx, sb, rz, rsp, rt, gn, st, so, g2, w2, gb, rxg, sx, rzh, hb, w3, w3x,
    eb, fr, fb, zr, stf, acc, ss,
):
    dp, hd = lax.axis_index("dp"), lax.axis_index("hd")
    x, zh = lax.rem(hd, NX), lax.div(hd, NX)
    c, z, y = lax.rem(dp, 2), lax.rem(lax.div(dp, 2), NZ), lax.div(dp, 2 * NZ)
    o = 1 - c

    def at(x_=x, zh_=zh, y_=y, z_=z, c_=c):
        return ((y_ * NZ + z_) * 2 + c_, zh_ * NX + x_)

    def plus(v, d, n):
        return lax.rem(v + d, n)

    used = [0]
    ends = []

    def sems(n):
        first = used[0]
        used[0] += n
        return first

    def copy(src, dst, send, recv, dev):
        return pltpu.make_async_remote_copy(
            src_ref=src, dst_ref=dst, send_sem=ss.at[send], recv_sem=ss.at[recv],
            device_id=dev, device_id_type=MESH,
        )

    def go(src, dst, send, recv, dev):
        copy(src, dst, send, recv, dev).start()

    def arrive(ref, recv):
        copy(ref, ref, recv, recv, peer).wait_recv()

    def sending(ref, when=None):
        send = sems(1)
        ends.append((when, ref, send))
        return send

    barrier = pltpu.get_barrier_semaphore()
    peer = at(c_=o)
    barrier = pltpu.get_barrier_semaphore()
    partners = []
    for d in (8, 7, 9, 6, 10, 5, 11, 4, 12, 3, 13, 2, 14, 1, 15):
        z16 = plus(zh * NZ + z, d, 16)
        partners.append(at(zh_=lax.div(z16, NZ), z_=lax.rem(z16, NZ)))
    for d in range(15, 0, -1):
        partners.append(at(x_=plus(x, d % 4, NX), y_=plus(y, d // 4, NY)))
    partners.append(peer)
    partners += [at(x_=plus(x, d, NX), c_=o) for d in (1, 2, 3)]
    for dev in partners[:15]:
        pl.semaphore_signal(barrier, inc=1, device_id=dev, device_id_type=MESH)

    loads = {}
    pairs = (
        (query_h, query), (cache_h, cache), (value_h, value_up), (res_h, residual), (gain_h, norm_gain),
        (proj_h, out_proj), (gate_h, gate_w), (up_h, up_w), (down_h, down_w), (lengths_h, lengths), (counts_h, counts),
    )
    for i, (src, dst) in enumerate(pairs):
        loads[i] = pltpu.make_async_copy(src, dst, ls.at[i])
        loads[i].start()
    for dev in partners[15:]:
        pl.semaphore_signal(barrier, inc=1, device_id=dev, device_id_type=MESH)

    loads[9].wait()
    row = lax.broadcasted_iota(jnp.int32, (64, POS), 0)
    pos = lax.broadcasted_iota(jnp.int32, (64, POS), 1)
    limit = lax.rem(lax.div(row, HEADS), QTOK) - 1
    for i in range(SLOTS):
        limit = limit + jnp.where(lax.div(row, 16) == i, lengths[i], 0)
    loads[0].wait()
    loads[1].wait()
    sc = [dot_t(query[i], cache[i]) for i in range(SLOTS)]
    sc = jnp.concatenate(sc, axis=0) * F32(192.0**-0.5)
    sc = jnp.where(pos < limit, sc, -1e30)
    ex = jnp.exp(sc - jnp.max(sc, axis=-1, keepdims=True))
    wt = (ex / jnp.sum(ex, axis=-1, keepdims=True)).astype(BF16)
    for i in range(SLOTS):
        la = jnp.dot(wt[16 * i : 16 * i + 16], cache[i, :, :LAT], preferred_element_type=F32)
        la = la.astype(BF16).astype(F32)
        for k in range(4):
            lat[k, pl.ds(i * 16, 16), :] = la[:, k * 128 : (k + 1) * 128]
    loads[2].wait()
    loads[10].wait()
    count = counts[0, 0]
    row8 = lax.broadcasted_iota(jnp.int32, (8, 128), 0)
    live = jnp.where(lax.div(row8, QTOK) < count, F32(1), F32(0))
    for h in range(HEADS):
        lh = [lat[k, pl.ds(h, 8, stride=HEADS), :] for k in range(4)]
        lh = jnp.concatenate(lh, axis=1).astype(BF16)
        hv = jnp.dot(lh, value_up[h], preferred_element_type=F32) * live
        hsc[h // 4, :, (h % 4) * 128 : (h % 4 + 1) * 128] = hv.astype(BF16).astype(F32)

    loads[3].wait()
    loads[4].wait()
    res = residual[...].astype(F32)
    gain = jnp.concatenate([norm_gain[i : i + 1, :] for i in range(7)], axis=1)
    rsp[...] = jnp.zeros_like(rsp)
    gn[...] = jnp.zeros_like(gn)
    for b in range(8):
        lo = (b // 2) * 128
        rsp[b % 2, :, lo : lo + OUTCOL] = res[:, b * OUTCOL : (b + 1) * OUTCOL]
        gn[b % 2, :, lo : lo + OUTCOL] = gain[:, b * OUTCOL : (b + 1) * OUTCOL]

    w1[...] = jnp.zeros_like(w1)
    loads[5].wait()
    w1[:OUTCOL, :] = out_proj[:, :512]
    w1[128 : 128 + OUTCOL, :] = out_proj[:, 512:]

    pl.semaphore_wait(barrier, len(partners))

    g1[c, y, z] = hsc[...].reshape(16, 512).astype(BF16)

    def gather_z(g):
        send, recv = sending(g.at[0, 0, pl.ds(0, 7)]), sems(3)
        for i in range(6, -1, -1):
            t = i + jnp.where(z <= i, 1, 0)
            high, low = apart(z, t, 4), apart(z, t, 2)
            go(g.at[c, y, z], g.at[c, y, z], send, recv + high * (1 + low), at(z_=t))
        return recv

    def gather_y(g, zrecv, consume, finish):
        ysend, csend, yrecv, crecv = sending(g.at[0, pl.ds(0, 3)]), sending(g.at[0]), sems(9), sems(4)
        parts = ((lax.div(z, 4) * 4, 4), (lax.div(flip(z, 4), 2) * 2, 2), (lax.div(flip(z, 6), 2) * 2, 2))
        for gi, (base, n) in enumerate(parts):
            arrive(g.at[c, y, pl.ds(base, n if gi else 3)], zrecv + gi)
            part = g.at[c, y, pl.ds(base, n)]
            for d in (2, 1, 3):
                go(part, part, ysend, yrecv + gi * 3 + d - 1, at(y_=plus(y, d, NY)))
            go(part, part, csend, crecv, peer)

        def forward(d):
            yd = plus(y, NY - d, NY)
            for gi, (base, n) in enumerate(parts):
                part = g.at[c, yd, pl.ds(base, n)]
                arrive(part, yrecv + gi * 3 + d - 1)
                go(part, part, csend, crecv + d, peer)

        def take(d):
            yd = plus(y, NY - d, NY)
            first = consume(g[c, yd].reshape(128, 512), c)
            arrive(g.at[o, yd], crecv + d)
            finish(first, consume(g[o, yd].reshape(128, 512), o), yd, d)

        return forward, take

    zin = gather_z(g1)
    res_in = sems(1)
    go(rsp.at[o], rt.at[c], sending(rsp.at[0]), res_in, peer)
    rt[c] = rsp[c]

    w2[...] = jnp.zeros_like(w2)
    loads[6].wait()
    loads[7].wait()
    for b in range(8):
        lo = (b // 2) * 128
        w2[b % 2, :UNITS, lo : lo + OUTCOL] = gate_w[:, b * OUTCOL : (b + 1) * OUTCOL]
        w2[b % 2, UNITS : 2 * UNITS, lo : lo + OUTCOL] = up_w[:, b * OUTCOL : (b + 1) * OUTCOL]
    r_ = lax.broadcasted_iota(jnp.int32, (16, 128), 0)
    c_ = lax.broadcasted_iota(jnp.int32, (16, 128), 1)
    ones = jnp.where((r_ == 0) & (c_ >= OUTCOL) & (c_ < OUTCOL + 2), F32(1), F32(0)).astype(BF16)
    for k in range(2):
        w2[k, 2 * UNITS : 2 * UNITS + 16, :128] = ones
    mine = c * NX + x
    for d in range(NY):
        hb[d, mine, :, 256:] = jnp.zeros((32, 128), BF16)

    xt = lax.rem(y, 2) * 2 + lax.div(z, 4)
    here = x == xt
    slot = lax.div(y, 2) * 4 + x
    psend, pself, precv = sending(pb.at[pl.ds(0, 3)]), sending(pb.at[0], jnp.logical_not(here)), sems(2)

    def project(block, k):
        both = dot_t(block, w1[...]).reshape(NZ, 16, 256)
        return both[:, :8, :128] + both[:, 8:, 128:]

    def out_projection(first, second, yd, d):
        pv = jnp.stack([jnp.where(c == 0, first, second), jnp.where(c == 0, second, first)], axis=1)
        pb[yd] = pv.reshape(NZ, 16, 128).astype(BF16)
        cp = copy(pb.at[yd], rx.at[slot], psend if d else pself, precv + lax.div(y, 2), at(x_=xt, y_=yd))
        if d:
            cp.start()
        else:
            pl.when(jnp.logical_not(here))(cp.start)

            @pl.when(here)
            def _():
                rx[slot] = pb[yd]

    forward, take = gather_y(g1, zin, project, out_projection)
    take(0)
    forward(1)
    forward(3)
    take(1)
    forward(2)
    take(3)
    take(2)

    holder = lax.rem(x, 2) == lax.div(z, 4)
    own = jnp.logical_and(holder, lax.rem(y, 2) == lax.div(x, 2))
    zsend, zrecv = sending(sb.at[pl.ds(0, 15)], holder), sems(1)
    z16 = zh * NZ + z
    myslot = zh * 4 + lax.rem(z, 4)

    for k in (1, 0):

        @pl.when(holder)
        def _():
            is_self = jnp.logical_and(own, lax.div(y, 2) == k)
            pl.when(is_self)(lambda: arrive(rx.at[pl.ds(0, 3)], precv + k))
            pl.when(jnp.logical_not(is_self))(lambda: arrive(rx.at[pl.ds(0, 4)], precv + k))
            tot = rx[4 * k].astype(F32) + rx[4 * k + 1].astype(F32)
            tot = tot + rx[4 * k + 2].astype(F32) + rx[4 * k + 3].astype(F32)
            sb[pl.ds(8 * k, 8)] = tot.astype(BF16)
            for zd in (0, 7, 1, 6, 2, 5, 3, 4):
                cp = copy(sb.at[8 * k + zd], rz.at[myslot], zsend, zrecv, at(zh_=k, z_=zd))
                pl.when(z16 != 8 * k + zd)(cp.start)

    @pl.when(holder)
    def _():
        rz[myslot] = sb[z16]

    w3[...] = jnp.zeros_like(w3)
    loads[8].wait()
    w3[0, :UNITS, :] = down_w[:, :512]
    w3[1, :UNITS, :384] = down_w[:, 512:]
    w3_in = sems(1)
    go(w3.at[o], w3x, sending(w3x), w3_in, peer)
    pl.when(holder)(lambda: arrive(rz.at[pl.ds(0, 7)], zrecv))
    pl.when(jnp.logical_not(holder))(lambda: arrive(rz, zrecv))

    arrive(rt.at[c], res_in)
    tiles = []
    for b in range(4):
        attn = (rz[b].astype(F32) + rz[4 + b].astype(F32)).astype(BF16).astype(F32)
        tiles.append(attn)
    attn = jnp.concatenate(tiles, axis=1)
    state = (rt[...].reshape(16, 512) + attn).astype(BF16).astype(F32)
    square = jnp.sum(state * state, axis=1, keepdims=True)
    high = square.astype(BF16).astype(F32)
    low = square - high
    scaled = state * gn[c]
    lane = lax.broadcasted_iota(jnp.int32, (16, 512), 1)
    scaled = jnp.where(lane == OUTCOL, high, jnp.where(lane == OUTCOL + 1, low, scaled))
    g2[c, y, z] = scaled.astype(BF16)
    zin = gather_z(g2)
    st[...] = state.reshape(2, 8, 512)
    st_in = sems(1)
    go(st.at[o], so.at[c], sending(st.at[0]), st_in, peer)
    so[c] = st[c]

    gsend, grecv = sending(gb.at[pl.ds(0, 3)]), sems(4)

    def gate_up_half(block, k):
        return dot_t(block, w2[k])

    def gate_up(first, second, yd, d):
        gb[d] = (first + second).astype(BF16).reshape(NX, 32, 640)
        for e in (1, 3, 2):
            xd = plus(x, e, NX)
            go(gb.at[d, xd], rxg.at[d, e - 1], gsend, grecv + d, at(x_=xd))

    hsend, hrecv = sending(sx), sems(4)
    other = at(zh_=1 - zh)

    def sum_x(d):
        tot = gb[d, x].astype(F32)
        arrive(rxg.at[d], grecv + d)
        for e in (1, 3, 2):
            tot = tot + rxg[d, e - 1].astype(F32)
        sx[d] = tot.astype(BF16)
        go(sx.at[d], rzh.at[d], hsend, hrecv + d, other)

    asend, arecv = [sending(hb.at[0, pl.ds(0, 7)]) for _ in range(NY)], sems(4)

    def hidden_units(d):
        arrive(rzh.at[d], hrecv + d)
        gu = sx[d].astype(F32) + rzh[d].astype(F32)
        inv = lax.rsqrt(gu[:, 2 * UNITS : 2 * UNITS + 1] / D + 1e-06)
        gate, up = gu[:, :UNITS] * inv, gu[:, UNITS : 2 * UNITS] * inv
        hid = gate / (1.0 + jnp.exp(-gate)) * up
        hb[d, mine, :, :UNITS] = hid.astype(BF16)
        for e in (2, 1, 3, 0):
            for dev in (at(x_=plus(x, e, NX)), at(x_=plus(x, e, NX), c_=o))[e == 0 :]:
                go(hb.at[d, mine], hb.at[d, mine], asend[d], arecv + d, dev)

    fsend, frecv = sending(eb), sems(1)

    def down(d):
        arrive(hb.at[d, pl.ds(0, 7)], arecv + d)
        own_, other_ = hb[d, pl.ds(c * NX, NX)].reshape(128, 384), hb[d, pl.ds(o * NX, NX)].reshape(128, 384)
        part = jnp.dot(own_, w3[c], preferred_element_type=F32)
        part = part + jnp.dot(other_, w3x[...], preferred_element_type=F32)
        if d == 0:
            acc[...] = part.reshape(NZ, 16, 512)
        else:
            eb[d - 1] = part.astype(BF16).reshape(NZ, 16, 512)
            go(eb.at[d - 1], fr.at[d - 1], fsend, frecv, at(y_=plus(y, NY - d, NY)))

    forward, take = gather_y(g2, zin, gate_up_half, gate_up)
    take(0)
    forward(1)
    forward(3)
    take(1)
    sum_x(0)
    forward(2)
    take(3)
    take(2)
    sum_x(1)
    sum_x(3)
    sum_x(2)
    hidden_units(0)
    arrive(w3x, w3_in)
    hidden_units(1)
    hidden_units(3)
    down(0)
    hidden_units(2)
    down(1)
    down(3)
    down(2)

    arrive(so.at[c], st_in)
    for b in range(8):
        lo = (b // 2) * 128
        stf[:, b * OUTCOL : (b + 1) * OUTCOL] = so[b % 2, :, lo : lo + OUTCOL]

    arrive(fr, frecv)
    oout, oin = sending(fb.at[pl.ds(0, 15)]), sems(1)

    def sum_y(t):
        return acc[t] + fr[0, t].astype(F32) + fr[1, t].astype(F32) + fr[2, t].astype(F32)

    def last_sum(t):
        tot = sum_y(t).astype(BF16).astype(F32)
        for k in range(2):
            rows = tot[8 * k : 8 * k + 8]
            fb[2 * t + k] = jnp.concatenate([rows[:, :256], rows[:, 256:]], axis=0).astype(BF16)

    me = 2 * z + c
    for i in range(7):
        t = i + jnp.where(z <= i, 1, 0)
        last_sum(t)
        for k in range(2):
            go(fb.at[2 * t + k], zr.at[me], oout, oin, at(z_=t, c_=k))
    last_sum(z)
    go(fb.at[2 * z + o], zr.at[me], oout, oin, peer)
    zr[me] = fb[me]
    arrive(zr.at[pl.ds(0, 15)], oin)
    cols = []
    for k in range(2):
        tot = zr[k].astype(F32)
        for j in range(1, 8):
            tot = tot + zr[2 * j + k].astype(F32)
        cols.append(jnp.concatenate([tot[:8], tot[8:]], axis=1))
    livew = live[:, :1]
    out[:, :512] = ((stf[:, :512] + cols[0]) * livew).astype(BF16)
    out[:, 512:] = ((stf[:, 512:] + cols[1][:, :384]) * livew).astype(BF16)

    for when, ref, send in ends:
        if when is None:
            copy(ref, ref, send, send, peer).wait_send()
        else:
            pl.when(when)(lambda ref=ref, send=send: copy(ref, ref, send, send, peer).wait_send())
    assert used[0] == NSEM, used


def per_device(query, cache, lengths, counts, value_up, out_proj, residual, norm_gain, gate_w, up_w, down_w):
    hbm = pl.BlockSpec(memory_space=pltpu.HBM)
    vmem = pl.BlockSpec(memory_space=pltpu.VMEM)
    b, f = lambda *s: pltpu.VMEM(s, BF16), lambda *s: pltpu.VMEM(s, F32)
    return pl.pallas_call(
        kernel,
        out_shape=jax.ShapeDtypeStruct((8, FEAT), BF16),
        in_specs=[hbm] * 11,
        out_specs=vmem,
        scratch_shapes=[
            b(SLOTS, 16, QK), b(SLOTS, POS, QK), pltpu.SMEM((4,), jnp.int32), pltpu.SMEM((1, 1), jnp.int32), b(HEADS, LAT, 128), b(OUTCOL, 1024), b(8, FEAT), f(7, 128),
            b(UNITS, FEAT), b(UNITS, FEAT), b(UNITS, FEAT), pltpu.SemaphoreType.DMA((11,)),
            f(4, 64, 128), f(2, 8, 512), b(2, NY, NZ, 16, 512), b(256, 512),
            b(NY, NZ, 16, 128), b(8, NZ, 16, 128), b(16, 16, 128), b(8, 16, 128),
            f(2, 8, 512), f(2, 8, 512), f(2, 1, 512), f(2, 8, 512), f(2, 8, 512),
            b(2, NY, NZ, 16, 512), b(2, 640, 512), b(NY, NX, 32, 640), b(NY, 3, 32, 640),
            b(NY, 32, 640), b(NY, 32, 640), b(NY, 2 * NX, 32, 384), b(2, 384, 512), b(384, 512),
            b(3, NZ, 16, 512), b(3, NZ, 16, 512),
            b(16, 16, 256), b(16, 16, 256), f(8, FEAT), f(NZ, 16, 512),
            pltpu.SemaphoreType.DMA((NSEM,)),
        ],
        compiler_params=pltpu.CompilerParams(
            collective_id=0, has_side_effects=True, vmem_limit_bytes=60 << 20
        ),
        name="decode_layer",
    )(
        query.reshape(SLOTS, QTOK * HEADS, QK), cache, lengths, counts.reshape(1, 1), value_up, out_proj.T, residual,
        norm_gain.reshape(7, 128), gate_w.T, up_w.T, down_w,
    )


def solution(mesh):
    return jax.shard_map(
        per_device,
        mesh=mesh,
        in_specs=(
            P("dp", None, "hd", None), P("dp", None, None), P("dp"), P("dp"), P("hd", None, None), P("hd", "dp"),
            P("dp", "hd"), P("hd"), P("hd", "dp"), P("hd", "dp"), P("dp", "hd"),
        ),
        out_specs=P("dp", "hd"),
        check_vma=False,
    )
```

```python
import functools

import jax
import jax.numpy as jnp
from jax import lax
from jax.experimental import pallas as pl
from jax.experimental.pallas import tpu as pltpu
from jax.sharding import PartitionSpec as P

MESH = pl.DeviceIdType.MESH
F32, BF16 = jnp.float32, jnp.bfloat16
D = 7168
SLOTS, QTOK, HEADS, LAT, QK, POS = 4, 2, 8, 512, 576, 192
NX, NY, NZ, NSEM = 4, 4, 8, 72
OUTCOL, FEAT, UNITS = 112, 896, 288


def flip(value, mask, bits=3):
    out = 0
    for i in range(bits):
        bit = lax.rem(lax.div(value, 1 << i), 2)
        out = out + (1 - bit if (mask >> i) & 1 else bit) * (1 << i)
    return out


def apart(a, b, unit):
    p, q = lax.rem(lax.div(a, unit), 2), lax.rem(lax.div(b, unit), 2)
    return p + q - 2 * p * q


def dot_t(a, b):
    return lax.dot_general(a, b, (((1,), (1,)), ((), ())), preferred_element_type=F32)


def kernel(
    query_h, cache_h, lengths_h, counts_h, value_h, proj_h, res_h, gain_h, gate_h, up_h, down_h,
    out,
    query, cache, lengths, counts, value_up, out_proj, residual, norm_gain, gate_w, up_w, down_w, ls,
    lat, hsc, g1, w1, pb, rx, sb, rz, rsp, rt, gn, st, so, g2, w2, gb, rxg, sx, rzh, hb, w3, w3x,
    eb, fr, fb, zr, stf, acc, ss,
):
    dp, hd = lax.axis_index("dp"), lax.axis_index("hd")
    x, zh = lax.rem(hd, NX), lax.div(hd, NX)
    c, z, y = lax.rem(dp, 2), lax.rem(lax.div(dp, 2), NZ), lax.div(dp, 2 * NZ)
    o = 1 - c

    def at(x_=x, zh_=zh, y_=y, z_=z, c_=c):
        return ((y_ * NZ + z_) * 2 + c_, zh_ * NX + x_)

    def plus(v, d, n):
        return lax.rem(v + d, n)

    used = [0]
    ends = []

    def sems(n):
        first = used[0]
        used[0] += n
        return first

    def copy(src, dst, send, recv, dev):
        return pltpu.make_async_remote_copy(
            src_ref=src, dst_ref=dst, send_sem=ss.at[send], recv_sem=ss.at[recv],
            device_id=dev, device_id_type=MESH,
        )

    def go(src, dst, send, recv, dev):
        copy(src, dst, send, recv, dev).start()

    def arrive(ref, recv):
        copy(ref, ref, recv, recv, peer).wait_recv()

    def sending(ref, when=None):
        send = sems(1)
        ends.append((when, ref, send))
        return send

    barrier = pltpu.get_barrier_semaphore()
    peer = at(c_=o)
    barrier = pltpu.get_barrier_semaphore()
    partners = []
    for d in (8, 7, 9, 6, 10, 5, 11, 4, 12, 3, 13, 2, 14, 1, 15):
        z16 = plus(zh * NZ + z, d, 16)
        partners.append(at(zh_=lax.div(z16, NZ), z_=lax.rem(z16, NZ)))
    for d in range(15, 0, -1):
        partners.append(at(x_=plus(x, d % 4, NX), y_=plus(y, d // 4, NY)))
    partners.append(peer)
    partners += [at(x_=plus(x, d, NX), c_=o) for d in (1, 2, 3)]
    for dev in partners[:15]:
        pl.semaphore_signal(barrier, inc=1, device_id=dev, device_id_type=MESH)

    loads = {}
    pairs = (
        (query_h, query), (cache_h, cache), (value_h, value_up), (res_h, residual), (gain_h, norm_gain),
        (proj_h, out_proj), (gate_h, gate_w), (up_h, up_w), (down_h, down_w), (lengths_h, lengths), (counts_h, counts),
    )
    for i, (src, dst) in enumerate(pairs):
        loads[i] = pltpu.make_async_copy(src, dst, ls.at[i])
        loads[i].start()
    for dev in partners[15:]:
        pl.semaphore_signal(barrier, inc=1, device_id=dev, device_id_type=MESH)

    loads[9].wait()
    row = lax.broadcasted_iota(jnp.int32, (64, POS), 0)
    pos = lax.broadcasted_iota(jnp.int32, (64, POS), 1)
    limit = lax.rem(lax.div(row, HEADS), QTOK) - 1
    for i in range(SLOTS):
        limit = limit + jnp.where(lax.div(row, 16) == i, lengths[i], 0)
    loads[0].wait()
    loads[1].wait()
    sc = [dot_t(query[i], cache[i]) for i in range(SLOTS)]
    sc = jnp.concatenate(sc, axis=0) * F32(192.0**-0.5)
    sc = jnp.where(pos < limit, sc, -1e30)
    ex = jnp.exp(sc - jnp.max(sc, axis=-1, keepdims=True))
    wt = (ex / jnp.sum(ex, axis=-1, keepdims=True)).astype(BF16)
    for i in range(SLOTS):
        la = jnp.dot(wt[16 * i : 16 * i + 16], cache[i, :, :LAT], preferred_element_type=F32)
        la = la.astype(BF16).astype(F32)
        for k in range(4):
            lat[k, pl.ds(i * 16, 16), :] = la[:, k * 128 : (k + 1) * 128]
    loads[2].wait()
    loads[10].wait()
    count = counts[0, 0]
    row8 = lax.broadcasted_iota(jnp.int32, (8, 128), 0)
    live = jnp.where(lax.div(row8, QTOK) < count, F32(1), F32(0))
    for h in range(HEADS):
        lh = [lat[k, pl.ds(h, 8, stride=HEADS), :] for k in range(4)]
        lh = jnp.concatenate(lh, axis=1).astype(BF16)
        hv = jnp.dot(lh, value_up[h], preferred_element_type=F32) * live
        hsc[h // 4, :, (h % 4) * 128 : (h % 4 + 1) * 128] = hv.astype(BF16).astype(F32)

    loads[3].wait()
    loads[4].wait()
    res = residual[...].astype(F32)
    gain = jnp.concatenate([norm_gain[i : i + 1, :] for i in range(7)], axis=1)
    rsp[...] = jnp.zeros_like(rsp)
    gn[...] = jnp.zeros_like(gn)
    for b in range(8):
        lo = (b // 2) * 128
        rsp[b % 2, :, lo : lo + OUTCOL] = res[:, b * OUTCOL : (b + 1) * OUTCOL]
        gn[b % 2, :, lo : lo + OUTCOL] = gain[:, b * OUTCOL : (b + 1) * OUTCOL]

    w1[...] = jnp.zeros_like(w1)
    loads[5].wait()
    w1[:OUTCOL, :] = out_proj[:, :512]
    w1[128 : 128 + OUTCOL, :] = out_proj[:, 512:]

    pl.semaphore_wait(barrier, len(partners))

    g1[c, y, z] = hsc[...].reshape(16, 512).astype(BF16)

    def gather_z(g):
        send, recv = sending(g.at[0, 0, pl.ds(0, 7)]), sems(3)
        for i in range(6, -1, -1):
            t = i + jnp.where(z <= i, 1, 0)
            high, low = apart(z, t, 4), apart(z, t, 2)
            go(g.at[c, y, z], g.at[c, y, z], send, recv + high * (1 + low), at(z_=t))
        return recv

    def gather_y(g, zrecv, consume, finish):
        ysend, csend, yrecv, crecv = sending(g.at[0, pl.ds(0, 3)]), sending(g.at[0]), sems(9), sems(4)
        parts = ((lax.div(z, 4) * 4, 4), (lax.div(flip(z, 4), 2) * 2, 2), (lax.div(flip(z, 6), 2) * 2, 2))
        for gi, (base, n) in enumerate(parts):
            arrive(g.at[c, y, pl.ds(base, n if gi else 3)], zrecv + gi)
            part = g.at[c, y, pl.ds(base, n)]
            for d in (1, 3, 2):
                go(part, part, ysend, yrecv + gi * 3 + d - 1, at(y_=plus(y, d, NY)))
            go(part, part, csend, crecv, peer)

        def forward(d):
            yd = plus(y, NY - d, NY)
            for gi, (base, n) in enumerate(parts):
                part = g.at[c, yd, pl.ds(base, n)]
                arrive(part, yrecv + gi * 3 + d - 1)
                go(part, part, csend, crecv + d, peer)

        def take(d):
            yd = plus(y, NY - d, NY)
            first = consume(g[c, yd].reshape(128, 512), c)
            arrive(g.at[o, yd], crecv + d)
            finish(first, consume(g[o, yd].reshape(128, 512), o), yd, d)

        return forward, take

    zin = gather_z(g1)
    res_in = sems(1)
    go(rsp.at[o], rt.at[c], sending(rsp.at[0]), res_in, peer)
    rt[c] = rsp[c]

    w2[...] = jnp.zeros_like(w2)
    loads[6].wait()
    loads[7].wait()
    for b in range(8):
        lo = (b // 2) * 128
        w2[b % 2, :UNITS, lo : lo + OUTCOL] = gate_w[:, b * OUTCOL : (b + 1) * OUTCOL]
        w2[b % 2, UNITS : 2 * UNITS, lo : lo + OUTCOL] = up_w[:, b * OUTCOL : (b + 1) * OUTCOL]
    r_ = lax.broadcasted_iota(jnp.int32, (16, 128), 0)
    c_ = lax.broadcasted_iota(jnp.int32, (16, 128), 1)
    ones = jnp.where((r_ == 0) & (c_ >= OUTCOL) & (c_ < OUTCOL + 2), F32(1), F32(0)).astype(BF16)
    for k in range(2):
        w2[k, 2 * UNITS : 2 * UNITS + 16, :128] = ones
    mine = c * NX + x
    for d in range(NY):
        hb[d, mine, :, 256:] = jnp.zeros((32, 128), BF16)

    xt = lax.rem(y, 2) * 2 + lax.div(z, 4)
    here = x == xt
    slot = lax.div(y, 2) * 4 + x
    psend, pself, precv = sending(pb.at[pl.ds(0, 3)]), sending(pb.at[0], jnp.logical_not(here)), sems(2)

    def project(block, k):
        both = dot_t(block, w1[...]).reshape(NZ, 16, 256)
        return both[:, :8, :128] + both[:, 8:, 128:]

    def out_projection(first, second, yd, d):
        pv = jnp.stack([jnp.where(c == 0, first, second), jnp.where(c == 0, second, first)], axis=1)
        pb[yd] = pv.reshape(NZ, 16, 128).astype(BF16)
        cp = copy(pb.at[yd], rx.at[slot], psend if d else pself, precv + lax.div(y, 2), at(x_=xt, y_=yd))
        if d:
            cp.start()
        else:
            pl.when(jnp.logical_not(here))(cp.start)

            @pl.when(here)
            def _():
                rx[slot] = pb[yd]

    forward, take = gather_y(g1, zin, project, out_projection)
    take(0)
    forward(1)
    forward(3)
    forward(2)
    take(1)
    take(3)
    take(2)

    holder = lax.rem(x, 2) == lax.div(z, 4)
    own = jnp.logical_and(holder, lax.rem(y, 2) == lax.div(x, 2))
    zsend, zrecv = sending(sb.at[pl.ds(0, 15)], holder), sems(1)
    z16 = zh * NZ + z
    myslot = zh * 4 + lax.rem(z, 4)

    for k in (1, 0):

        @pl.when(holder)
        def _():
            is_self = jnp.logical_and(own, lax.div(y, 2) == k)
            pl.when(is_self)(lambda: arrive(rx.at[pl.ds(0, 3)], precv + k))
            pl.when(jnp.logical_not(is_self))(lambda: arrive(rx.at[pl.ds(0, 4)], precv + k))
            tot = rx[4 * k].astype(F32) + rx[4 * k + 1].astype(F32)
            tot = tot + rx[4 * k + 2].astype(F32) + rx[4 * k + 3].astype(F32)
            sb[pl.ds(8 * k, 8)] = tot.astype(BF16)
            for zd in (0, 7, 1, 6, 2, 5, 3, 4):
                cp = copy(sb.at[8 * k + zd], rz.at[myslot], zsend, zrecv, at(zh_=k, z_=zd))
                pl.when(z16 != 8 * k + zd)(cp.start)

    @pl.when(holder)
    def _():
        rz[myslot] = sb[z16]

    w3[...] = jnp.zeros_like(w3)
    loads[8].wait()
    w3[0, :UNITS, :] = down_w[:, :512]
    w3[1, :UNITS, :384] = down_w[:, 512:]
    w3_in = sems(1)
    go(w3.at[o], w3x, sending(w3x), w3_in, peer)
    pl.when(holder)(lambda: arrive(rz.at[pl.ds(0, 7)], zrecv))
    pl.when(jnp.logical_not(holder))(lambda: arrive(rz, zrecv))

    arrive(rt.at[c], res_in)
    tiles = []
    for b in range(4):
        attn = (rz[b].astype(F32) + rz[4 + b].astype(F32)).astype(BF16).astype(F32)
        tiles.append(attn)
    attn = jnp.concatenate(tiles, axis=1)
    state = (rt[...].reshape(16, 512) + attn).astype(BF16).astype(F32)
    square = jnp.sum(state * state, axis=1, keepdims=True)
    high = square.astype(BF16).astype(F32)
    low = square - high
    scaled = state * gn[c]
    lane = lax.broadcasted_iota(jnp.int32, (16, 512), 1)
    scaled = jnp.where(lane == OUTCOL, high, jnp.where(lane == OUTCOL + 1, low, scaled))
    g2[c, y, z] = scaled.astype(BF16)
    zin = gather_z(g2)
    st[...] = state.reshape(2, 8, 512)
    st_in = sems(1)
    go(st.at[o], so.at[c], sending(st.at[0]), st_in, peer)
    so[c] = st[c]

    gsend, grecv = sending(gb.at[pl.ds(0, 3)]), sems(4)

    def gate_up_half(block, k):
        return dot_t(block, w2[k])

    def gate_up(first, second, yd, d):
        gb[d] = (first + second).astype(BF16).reshape(NX, 32, 640)
        for e in (1, 3, 2):
            xd = plus(x, e, NX)
            go(gb.at[d, xd], rxg.at[d, e - 1], gsend, grecv + d, at(x_=xd))

    hsend, hrecv = sending(sx), sems(4)
    other = at(zh_=1 - zh)

    def sum_x(d):
        tot = gb[d, x].astype(F32)
        arrive(rxg.at[d], grecv + d)
        for e in (1, 3, 2):
            tot = tot + rxg[d, e - 1].astype(F32)
        sx[d] = tot.astype(BF16)
        go(sx.at[d], rzh.at[d], hsend, hrecv + d, other)

    asend, arecv = [sending(hb.at[0, pl.ds(0, 7)]) for _ in range(NY)], sems(4)

    def hidden_units(d):
        arrive(rzh.at[d], hrecv + d)
        gu = sx[d].astype(F32) + rzh[d].astype(F32)
        inv = lax.rsqrt(gu[:, 2 * UNITS : 2 * UNITS + 1] / D + 1e-06)
        gate, up = gu[:, :UNITS] * inv, gu[:, UNITS : 2 * UNITS] * inv
        hid = gate / (1.0 + jnp.exp(-gate)) * up
        hb[d, mine, :, :UNITS] = hid.astype(BF16)
        for e in (2, 1, 3, 0):
            for dev in (at(x_=plus(x, e, NX)), at(x_=plus(x, e, NX), c_=o))[e == 0 :]:
                go(hb.at[d, mine], hb.at[d, mine], asend[d], arecv + d, dev)

    fsend, frecv = sending(eb), sems(1)

    def down(d):
        arrive(hb.at[d, pl.ds(0, 7)], arecv + d)
        own_, other_ = hb[d, pl.ds(c * NX, NX)].reshape(128, 384), hb[d, pl.ds(o * NX, NX)].reshape(128, 384)
        part = jnp.dot(own_, w3[c], preferred_element_type=F32)
        part = part + jnp.dot(other_, w3x[...], preferred_element_type=F32)
        if d == 0:
            acc[...] = part.reshape(NZ, 16, 512)
        else:
            eb[d - 1] = part.astype(BF16).reshape(NZ, 16, 512)
            go(eb.at[d - 1], fr.at[d - 1], fsend, frecv, at(y_=plus(y, NY - d, NY)))

    forward, take = gather_y(g2, zin, gate_up_half, gate_up)
    take(0)
    forward(1)
    forward(3)
    forward(2)
    take(1)
    sum_x(0)
    take(3)
    take(2)
    sum_x(1)
    sum_x(3)
    sum_x(2)
    arrive(w3x, w3_in)
    hidden_units(0)
    hidden_units(1)
    hidden_units(3)
    hidden_units(2)
    down(1)
    down(3)
    down(2)
    down(0)

    arrive(so.at[c], st_in)
    for b in range(8):
        lo = (b // 2) * 128
        stf[:, b * OUTCOL : (b + 1) * OUTCOL] = so[b % 2, :, lo : lo + OUTCOL]

    arrive(fr, frecv)
    oout, oin = sending(fb.at[pl.ds(0, 15)]), sems(1)

    def sum_y(t):
        return acc[t] + fr[0, t].astype(F32) + fr[1, t].astype(F32) + fr[2, t].astype(F32)

    def last_sum(t):
        tot = sum_y(t).astype(BF16).astype(F32)
        for k in range(2):
            rows = tot[8 * k : 8 * k + 8]
            fb[2 * t + k] = jnp.concatenate([rows[:, :256], rows[:, 256:]], axis=0).astype(BF16)

    me = 2 * z + c
    for i in range(7):
        t = i + jnp.where(z <= i, 1, 0)
        last_sum(t)
        for k in range(2):
            go(fb.at[2 * t + k], zr.at[me], oout, oin, at(z_=t, c_=k))
    last_sum(z)
    go(fb.at[2 * z + o], zr.at[me], oout, oin, peer)
    zr[me] = fb[me]
    arrive(zr.at[pl.ds(0, 15)], oin)
    cols = []
    for k in range(2):
        tot = zr[k].astype(F32)
        for j in range(1, 8):
            tot = tot + zr[2 * j + k].astype(F32)
        cols.append(jnp.concatenate([tot[:8], tot[8:]], axis=1))
    livew = live[:, :1]
    out[:, :512] = ((stf[:, :512] + cols[0]) * livew).astype(BF16)
    out[:, 512:] = ((stf[:, 512:] + cols[1][:, :384]) * livew).astype(BF16)

    for when, ref, send in ends:
        if when is None:
            copy(ref, ref, send, send, peer).wait_send()
        else:
            pl.when(when)(lambda ref=ref, send=send: copy(ref, ref, send, send, peer).wait_send())
    assert used[0] == NSEM, used


def per_device(query, cache, lengths, counts, value_up, out_proj, residual, norm_gain, gate_w, up_w, down_w):
    hbm = pl.BlockSpec(memory_space=pltpu.HBM)
    vmem = pl.BlockSpec(memory_space=pltpu.VMEM)
    b, f = lambda *s: pltpu.VMEM(s, BF16), lambda *s: pltpu.VMEM(s, F32)
    return pl.pallas_call(
        kernel,
        out_shape=jax.ShapeDtypeStruct((8, FEAT), BF16),
        in_specs=[hbm] * 11,
        out_specs=vmem,
        scratch_shapes=[
            b(SLOTS, 16, QK), b(SLOTS, POS, QK), pltpu.SMEM((4,), jnp.int32), pltpu.SMEM((1, 1), jnp.int32), b(HEADS, LAT, 128), b(OUTCOL, 1024), b(8, FEAT), f(7, 128),
            b(UNITS, FEAT), b(UNITS, FEAT), b(UNITS, FEAT), pltpu.SemaphoreType.DMA((11,)),
            f(4, 64, 128), f(2, 8, 512), b(2, NY, NZ, 16, 512), b(256, 512),
            b(NY, NZ, 16, 128), b(8, NZ, 16, 128), b(16, 16, 128), b(8, 16, 128),
            f(2, 8, 512), f(2, 8, 512), f(2, 1, 512), f(2, 8, 512), f(2, 8, 512),
            b(2, NY, NZ, 16, 512), b(2, 640, 512), b(NY, NX, 32, 640), b(NY, 3, 32, 640),
            b(NY, 32, 640), b(NY, 32, 640), b(NY, 2 * NX, 32, 384), b(2, 384, 512), b(384, 512),
            b(3, NZ, 16, 512), b(3, NZ, 16, 512),
            b(16, 16, 256), b(16, 16, 256), f(8, FEAT), f(NZ, 16, 512),
            pltpu.SemaphoreType.DMA((NSEM,)),
        ],
        compiler_params=pltpu.CompilerParams(
            collective_id=0, has_side_effects=True, vmem_limit_bytes=60 << 20
        ),
        name="decode_layer",
    )(
        query.reshape(SLOTS, QTOK * HEADS, QK), cache, lengths, counts.reshape(1, 1), value_up, out_proj.T, residual,
        norm_gain.reshape(7, 128), gate_w.T, up_w.T, down_w,
    )


def solution(mesh):
    return jax.shard_map(
        per_device,
        mesh=mesh,
        in_specs=(
            P("dp", None, "hd", None), P("dp", None, None), P("dp"), P("dp"), P("hd", None, None), P("hd", "dp"),
            P("dp", "hd"), P("hd"), P("hd", "dp"), P("hd", "dp"), P("dp", "hd"),
        ),
        out_specs=P("dp", "hd"),
        check_vma=False,
    )
```

```python
import functools

import jax
import jax.numpy as jnp
from jax import lax
from jax.experimental import pallas as pl
from jax.experimental.pallas import tpu as pltpu
from jax.sharding import PartitionSpec as P

MESH = pl.DeviceIdType.MESH
F32, BF16 = jnp.float32, jnp.bfloat16
D = 7168
SLOTS, QTOK, HEADS, LAT, QK, POS = 4, 2, 8, 512, 576, 192
NX, NY, NZ, NSEM = 4, 4, 8, 72
OUTCOL, FEAT, UNITS = 112, 896, 288


def flip(value, mask, bits=3):
    out = 0
    for i in range(bits):
        bit = lax.rem(lax.div(value, 1 << i), 2)
        out = out + (1 - bit if (mask >> i) & 1 else bit) * (1 << i)
    return out


def apart(a, b, unit):
    p, q = lax.rem(lax.div(a, unit), 2), lax.rem(lax.div(b, unit), 2)
    return p + q - 2 * p * q


def dot_t(a, b):
    return lax.dot_general(a, b, (((1,), (1,)), ((), ())), preferred_element_type=F32)


def kernel(
    query_h, cache_h, lengths_h, counts_h, value_h, proj_h, res_h, gain_h, gate_h, up_h, down_h,
    out,
    query, cache, lengths, counts, value_up, out_proj, residual, norm_gain, gate_w, up_w, down_w, ls,
    lat, hsc, g1, w1, pb, rx, sb, rz, rsp, rt, gn, st, so, g2, w2, gb, rxg, sx, rzh, hb, w3, w3x,
    eb, fr, fb, zr, stf, acc, ss,
):
    dp, hd = lax.axis_index("dp"), lax.axis_index("hd")
    x, zh = lax.rem(hd, NX), lax.div(hd, NX)
    c, z, y = lax.rem(dp, 2), lax.rem(lax.div(dp, 2), NZ), lax.div(dp, 2 * NZ)
    o = 1 - c

    def at(x_=x, zh_=zh, y_=y, z_=z, c_=c):
        return ((y_ * NZ + z_) * 2 + c_, zh_ * NX + x_)

    def plus(v, d, n):
        return lax.rem(v + d, n)

    used = [0]
    ends = []

    def sems(n):
        first = used[0]
        used[0] += n
        return first

    def copy(src, dst, send, recv, dev):
        return pltpu.make_async_remote_copy(
            src_ref=src, dst_ref=dst, send_sem=ss.at[send], recv_sem=ss.at[recv],
            device_id=dev, device_id_type=MESH,
        )

    def go(src, dst, send, recv, dev):
        copy(src, dst, send, recv, dev).start()

    def arrive(ref, recv):
        copy(ref, ref, recv, recv, peer).wait_recv()

    def sending(ref, when=None):
        send = sems(1)
        ends.append((when, ref, send))
        return send

    barrier = pltpu.get_barrier_semaphore()
    peer = at(c_=o)
    barrier = pltpu.get_barrier_semaphore()
    partners = []
    for d in (8, 7, 9, 6, 10, 5, 11, 4, 12, 3, 13, 2, 14, 1, 15):
        z16 = plus(zh * NZ + z, d, 16)
        partners.append(at(zh_=lax.div(z16, NZ), z_=lax.rem(z16, NZ)))
    for d in range(15, 0, -1):
        partners.append(at(x_=plus(x, d % 4, NX), y_=plus(y, d // 4, NY)))
    partners.append(peer)
    partners += [at(x_=plus(x, d, NX), c_=o) for d in (1, 2, 3)]
    for dev in partners[:15]:
        pl.semaphore_signal(barrier, inc=1, device_id=dev, device_id_type=MESH)

    loads = {}
    pairs = (
        (query_h, query), (cache_h, cache), (value_h, value_up), (res_h, residual), (gain_h, norm_gain),
        (proj_h, out_proj), (gate_h, gate_w), (up_h, up_w), (down_h, down_w), (lengths_h, lengths), (counts_h, counts),
    )
    for i, (src, dst) in enumerate(pairs):
        loads[i] = pltpu.make_async_copy(src, dst, ls.at[i])
        loads[i].start()
    for dev in partners[15:]:
        pl.semaphore_signal(barrier, inc=1, device_id=dev, device_id_type=MESH)

    loads[9].wait()
    row = lax.broadcasted_iota(jnp.int32, (64, POS), 0)
    pos = lax.broadcasted_iota(jnp.int32, (64, POS), 1)
    limit = lax.rem(lax.div(row, HEADS), QTOK) - 1
    for i in range(SLOTS):
        limit = limit + jnp.where(lax.div(row, 16) == i, lengths[i], 0)
    loads[0].wait()
    loads[1].wait()
    sc = [dot_t(query[i], cache[i]) for i in range(SLOTS)]
    sc = jnp.concatenate(sc, axis=0) * F32(192.0**-0.5)
    sc = jnp.where(pos < limit, sc, -1e30)
    ex = jnp.exp(sc - jnp.max(sc, axis=-1, keepdims=True))
    wt = (ex / jnp.sum(ex, axis=-1, keepdims=True)).astype(BF16)
    for i in range(SLOTS):
        la = jnp.dot(wt[16 * i : 16 * i + 16], cache[i, :, :LAT], preferred_element_type=F32)
        la = la.astype(BF16).astype(F32)
        for k in range(4):
            lat[k, pl.ds(i * 16, 16), :] = la[:, k * 128 : (k + 1) * 128]
    loads[2].wait()
    loads[10].wait()
    count = counts[0, 0]
    row8 = lax.broadcasted_iota(jnp.int32, (8, 128), 0)
    live = jnp.where(lax.div(row8, QTOK) < count, F32(1), F32(0))
    for h in range(HEADS):
        lh = [lat[k, pl.ds(h, 8, stride=HEADS), :] for k in range(4)]
        lh = jnp.concatenate(lh, axis=1).astype(BF16)
        hv = jnp.dot(lh, value_up[h], preferred_element_type=F32) * live
        hsc[h // 4, :, (h % 4) * 128 : (h % 4 + 1) * 128] = hv.astype(BF16).astype(F32)

    loads[3].wait()
    loads[4].wait()
    res = residual[...].astype(F32)
    gain = jnp.concatenate([norm_gain[i : i + 1, :] for i in range(7)], axis=1)
    rsp[...] = jnp.zeros_like(rsp)
    gn[...] = jnp.zeros_like(gn)
    for b in range(8):
        lo = (b // 2) * 128
        rsp[b % 2, :, lo : lo + OUTCOL] = res[:, b * OUTCOL : (b + 1) * OUTCOL]
        gn[b % 2, :, lo : lo + OUTCOL] = gain[:, b * OUTCOL : (b + 1) * OUTCOL]

    w1[...] = jnp.zeros_like(w1)
    loads[5].wait()
    w1[:OUTCOL, :] = out_proj[:, :512]
    w1[128 : 128 + OUTCOL, :] = out_proj[:, 512:]

    pl.semaphore_wait(barrier, len(partners))

    g1[c, y, z] = hsc[...].reshape(16, 512).astype(BF16)

    def gather_z(g):
        send, recv = sending(g.at[0, 0, pl.ds(0, 7)]), sems(3)
        for i in (6, 0, 5, 4, 3, 2, 1):
            t = i + jnp.where(z <= i, 1, 0)
            high, low = apart(z, t, 4), apart(z, t, 2)
            go(g.at[c, y, z], g.at[c, y, z], send, recv + high * (1 + low), at(z_=t))
        return recv

    def gather_y(g, zrecv, consume, finish):
        ysend, csend, yrecv, crecv = sending(g.at[0, pl.ds(0, 3)]), sending(g.at[0]), sems(9), sems(4)
        parts = ((lax.div(z, 4) * 4, 4), (lax.div(flip(z, 4), 2) * 2, 2), (lax.div(flip(z, 6), 2) * 2, 2))
        for gi, (base, n) in enumerate(parts):
            arrive(g.at[c, y, pl.ds(base, n if gi else 3)], zrecv + gi)
            part = g.at[c, y, pl.ds(base, n)]
            for d in (1, 3, 2):
                go(part, part, ysend, yrecv + gi * 3 + d - 1, at(y_=plus(y, d, NY)))
            go(part, part, csend, crecv, peer)

        def forward(d):
            yd = plus(y, NY - d, NY)
            for gi, (base, n) in enumerate(parts):
                part = g.at[c, yd, pl.ds(base, n)]
                arrive(part, yrecv + gi * 3 + d - 1)
                go(part, part, csend, crecv + d, peer)

        def take(d):
            yd = plus(y, NY - d, NY)
            first = consume(g[c, yd].reshape(128, 512), c)
            arrive(g.at[o, yd], crecv + d)
            finish(first, consume(g[o, yd].reshape(128, 512), o), yd, d)

        return forward, take

    zin = gather_z(g1)
    res_in = sems(1)
    go(rsp.at[o], rt.at[c], sending(rsp.at[0]), res_in, peer)
    rt[c] = rsp[c]

    w2[...] = jnp.zeros_like(w2)
    loads[6].wait()
    loads[7].wait()
    for b in range(8):
        lo = (b // 2) * 128
        w2[b % 2, :UNITS, lo : lo + OUTCOL] = gate_w[:, b * OUTCOL : (b + 1) * OUTCOL]
        w2[b % 2, UNITS : 2 * UNITS, lo : lo + OUTCOL] = up_w[:, b * OUTCOL : (b + 1) * OUTCOL]
    r_ = lax.broadcasted_iota(jnp.int32, (16, 128), 0)
    c_ = lax.broadcasted_iota(jnp.int32, (16, 128), 1)
    ones = jnp.where((r_ == 0) & (c_ >= OUTCOL) & (c_ < OUTCOL + 2), F32(1), F32(0)).astype(BF16)
    for k in range(2):
        w2[k, 2 * UNITS : 2 * UNITS + 16, :128] = ones
    mine = c * NX + x
    for d in range(NY):
        hb[d, mine, :, 256:] = jnp.zeros((32, 128), BF16)

    xt = lax.rem(y, 2) * 2 + lax.div(z, 4)
    here = x == xt
    slot = lax.div(y, 2) * 4 + x
    psend, pself, precv = sending(pb.at[pl.ds(0, 3)]), sending(pb.at[0], jnp.logical_not(here)), sems(2)

    def project(block, k):
        both = dot_t(block, w1[...]).reshape(NZ, 16, 256)
        return both[:, :8, :128] + both[:, 8:, 128:]

    def out_projection(first, second, yd, d):
        pv = jnp.stack([jnp.where(c == 0, first, second), jnp.where(c == 0, second, first)], axis=1)
        pb[yd] = pv.reshape(NZ, 16, 128).astype(BF16)
        cp = copy(pb.at[yd], rx.at[slot], psend if d else pself, precv + lax.div(y, 2), at(x_=xt, y_=yd))
        if d:
            cp.start()
        else:
            pl.when(jnp.logical_not(here))(cp.start)

            @pl.when(here)
            def _():
                rx[slot] = pb[yd]

    forward, take = gather_y(g1, zin, project, out_projection)
    take(0)
    forward(1)
    forward(3)
    forward(2)
    take(1)
    take(3)
    take(2)

    holder = lax.rem(x, 2) == lax.div(z, 4)
    own = jnp.logical_and(holder, lax.rem(y, 2) == lax.div(x, 2))
    zsend, zrecv = sending(sb.at[pl.ds(0, 15)], holder), sems(1)
    z16 = zh * NZ + z
    myslot = zh * 4 + lax.rem(z, 4)

    for k in (1, 0):

        @pl.when(holder)
        def _():
            is_self = jnp.logical_and(own, lax.div(y, 2) == k)
            pl.when(is_self)(lambda: arrive(rx.at[pl.ds(0, 3)], precv + k))
            pl.when(jnp.logical_not(is_self))(lambda: arrive(rx.at[pl.ds(0, 4)], precv + k))
            tot = rx[4 * k].astype(F32) + rx[4 * k + 1].astype(F32)
            tot = tot + rx[4 * k + 2].astype(F32) + rx[4 * k + 3].astype(F32)
            sb[pl.ds(8 * k, 8)] = tot.astype(BF16)
            for zd in (7, 0, 6, 1, 5, 2, 4, 3):
                cp = copy(sb.at[8 * k + zd], rz.at[myslot], zsend, zrecv, at(zh_=k, z_=zd))
                pl.when(z16 != 8 * k + zd)(cp.start)

    @pl.when(holder)
    def _():
        rz[myslot] = sb[z16]

    w3[...] = jnp.zeros_like(w3)
    loads[8].wait()
    w3[0, :UNITS, :] = down_w[:, :512]
    w3[1, :UNITS, :384] = down_w[:, 512:]
    w3_in = sems(1)
    go(w3.at[o], w3x, sending(w3x), w3_in, peer)
    pl.when(holder)(lambda: arrive(rz.at[pl.ds(0, 7)], zrecv))
    pl.when(jnp.logical_not(holder))(lambda: arrive(rz, zrecv))

    arrive(rt.at[c], res_in)
    tiles = []
    for b in range(4):
        attn = (rz[b].astype(F32) + rz[4 + b].astype(F32)).astype(BF16).astype(F32)
        tiles.append(attn)
    attn = jnp.concatenate(tiles, axis=1)
    state = (rt[...].reshape(16, 512) + attn).astype(BF16).astype(F32)
    square = jnp.sum(state * state, axis=1, keepdims=True)
    high = square.astype(BF16).astype(F32)
    low = square - high
    scaled = state * gn[c]
    lane = lax.broadcasted_iota(jnp.int32, (16, 512), 1)
    scaled = jnp.where(lane == OUTCOL, high, jnp.where(lane == OUTCOL + 1, low, scaled))
    g2[c, y, z] = scaled.astype(BF16)
    zin = gather_z(g2)
    st[...] = state.reshape(2, 8, 512)
    st_in = sems(1)
    go(st.at[o], so.at[c], sending(st.at[0]), st_in, peer)
    so[c] = st[c]

    gsend, grecv = sending(gb.at[pl.ds(0, 3)]), sems(4)

    def gate_up_half(block, k):
        return dot_t(block, w2[k])

    def gate_up(first, second, yd, d):
        gb[d] = (first + second).astype(BF16).reshape(NX, 32, 640)
        for e in (1, 3, 2):
            xd = plus(x, e, NX)
            go(gb.at[d, xd], rxg.at[d, e - 1], gsend, grecv + d, at(x_=xd))

    hsend, hrecv = sending(sx), sems(4)
    other = at(zh_=1 - zh)

    def sum_x(d):
        tot = gb[d, x].astype(F32)
        arrive(rxg.at[d], grecv + d)
        for e in (1, 3, 2):
            tot = tot + rxg[d, e - 1].astype(F32)
        sx[d] = tot.astype(BF16)
        go(sx.at[d], rzh.at[d], hsend, hrecv + d, other)

    asend, arecv = [sending(hb.at[0, pl.ds(0, 7)]) for _ in range(NY)], sems(4)

    def hidden_units(d):
        arrive(rzh.at[d], hrecv + d)
        gu = sx[d].astype(F32) + rzh[d].astype(F32)
        inv = lax.rsqrt(gu[:, 2 * UNITS : 2 * UNITS + 1] / D + 1e-06)
        gate, up = gu[:, :UNITS] * inv, gu[:, UNITS : 2 * UNITS] * inv
        hid = gate / (1.0 + jnp.exp(-gate)) * up
        hb[d, mine, :, :UNITS] = hid.astype(BF16)
        for e in (2, 1, 3, 0):
            for dev in (at(x_=plus(x, e, NX)), at(x_=plus(x, e, NX), c_=o))[e == 0 :]:
                go(hb.at[d, mine], hb.at[d, mine], asend[d], arecv + d, dev)

    fsend, frecv = sending(eb), sems(1)

    def down(d):
        arrive(hb.at[d, pl.ds(0, 7)], arecv + d)
        own_, other_ = hb[d, pl.ds(c * NX, NX)].reshape(128, 384), hb[d, pl.ds(o * NX, NX)].reshape(128, 384)
        part = jnp.dot(own_, w3[c], preferred_element_type=F32)
        part = part + jnp.dot(other_, w3x[...], preferred_element_type=F32)
        if d == 0:
            acc[...] = part.reshape(NZ, 16, 512)
        else:
            eb[d - 1] = part.astype(BF16).reshape(NZ, 16, 512)
            go(eb.at[d - 1], fr.at[d - 1], fsend, frecv, at(y_=plus(y, NY - d, NY)))

    forward, take = gather_y(g2, zin, gate_up_half, gate_up)
    take(0)
    forward(1)
    forward(3)
    forward(2)
    take(1)
    sum_x(0)
    take(3)
    take(2)
    sum_x(1)
    sum_x(3)
    sum_x(2)
    arrive(w3x, w3_in)
    hidden_units(0)
    hidden_units(1)
    hidden_units(3)
    hidden_units(2)
    down(1)
    down(3)
    down(2)
    down(0)

    arrive(so.at[c], st_in)
    for b in range(8):
        lo = (b // 2) * 128
        stf[:, b * OUTCOL : (b + 1) * OUTCOL] = so[b % 2, :, lo : lo + OUTCOL]

    arrive(fr, frecv)
    oout, oin = sending(fb.at[pl.ds(0, 15)]), sems(1)

    def sum_y(t):
        return acc[t] + fr[0, t].astype(F32) + fr[1, t].astype(F32) + fr[2, t].astype(F32)

    def last_sum(t):
        tot = sum_y(t).astype(BF16).astype(F32)
        for k in range(2):
            rows = tot[8 * k : 8 * k + 8]
            fb[2 * t + k] = jnp.concatenate([rows[:, :256], rows[:, 256:]], axis=0).astype(BF16)

    me = 2 * z + c
    for i in range(7):
        t = i + jnp.where(z <= i, 1, 0)
        last_sum(t)
        for k in range(2):
            go(fb.at[2 * t + k], zr.at[me], oout, oin, at(z_=t, c_=k))
    last_sum(z)
    go(fb.at[2 * z + o], zr.at[me], oout, oin, peer)
    zr[me] = fb[me]
    arrive(zr.at[pl.ds(0, 15)], oin)
    cols = []
    for k in range(2):
        tot = zr[k].astype(F32)
        for j in range(1, 8):
            tot = tot + zr[2 * j + k].astype(F32)
        cols.append(jnp.concatenate([tot[:8], tot[8:]], axis=1))
    livew = live[:, :1]
    out[:, :512] = ((stf[:, :512] + cols[0]) * livew).astype(BF16)
    out[:, 512:] = ((stf[:, 512:] + cols[1][:, :384]) * livew).astype(BF16)

    for when, ref, send in ends:
        if when is None:
            copy(ref, ref, send, send, peer).wait_send()
        else:
            pl.when(when)(lambda ref=ref, send=send: copy(ref, ref, send, send, peer).wait_send())
    assert used[0] == NSEM, used


def per_device(query, cache, lengths, counts, value_up, out_proj, residual, norm_gain, gate_w, up_w, down_w):
    hbm = pl.BlockSpec(memory_space=pltpu.HBM)
    vmem = pl.BlockSpec(memory_space=pltpu.VMEM)
    b, f = lambda *s: pltpu.VMEM(s, BF16), lambda *s: pltpu.VMEM(s, F32)
    return pl.pallas_call(
        kernel,
        out_shape=jax.ShapeDtypeStruct((8, FEAT), BF16),
        in_specs=[hbm] * 11,
        out_specs=vmem,
        scratch_shapes=[
            b(SLOTS, 16, QK), b(SLOTS, POS, QK), pltpu.SMEM((4,), jnp.int32), pltpu.SMEM((1, 1), jnp.int32), b(HEADS, LAT, 128), b(OUTCOL, 1024), b(8, FEAT), f(7, 128),
            b(UNITS, FEAT), b(UNITS, FEAT), b(UNITS, FEAT), pltpu.SemaphoreType.DMA((11,)),
            f(4, 64, 128), f(2, 8, 512), b(2, NY, NZ, 16, 512), b(256, 512),
            b(NY, NZ, 16, 128), b(8, NZ, 16, 128), b(16, 16, 128), b(8, 16, 128),
            f(2, 8, 512), f(2, 8, 512), f(2, 1, 512), f(2, 8, 512), f(2, 8, 512),
            b(2, NY, NZ, 16, 512), b(2, 640, 512), b(NY, NX, 32, 640), b(NY, 3, 32, 640),
            b(NY, 32, 640), b(NY, 32, 640), b(NY, 2 * NX, 32, 384), b(2, 384, 512), b(384, 512),
            b(3, NZ, 16, 512), b(3, NZ, 16, 512),
            b(16, 16, 256), b(16, 16, 256), f(8, FEAT), f(NZ, 16, 512),
            pltpu.SemaphoreType.DMA((NSEM,)),
        ],
        compiler_params=pltpu.CompilerParams(
            collective_id=0, has_side_effects=True, vmem_limit_bytes=60 << 20
        ),
        name="decode_layer",
    )(
        query.reshape(SLOTS, QTOK * HEADS, QK), cache, lengths, counts.reshape(1, 1), value_up, out_proj.T, residual,
        norm_gain.reshape(7, 128), gate_w.T, up_w.T, down_w,
    )


def solution(mesh):
    return jax.shard_map(
        per_device,
        mesh=mesh,
        in_specs=(
            P("dp", None, "hd", None), P("dp", None, None), P("dp"), P("dp"), P("hd", None, None), P("hd", "dp"),
            P("dp", "hd"), P("hd"), P("hd", "dp"), P("hd", "dp"), P("dp", "hd"),
        ),
        out_specs=P("dp", "hd"),
        check_vma=False,
    )
```
